256 devices in a mesh: ens: 4 (over x_hi, core), space: 64 (over x_lo, z, y).
Axes of the slice: x: 4 (x_hi: 2, x_lo: 2; x = x_hi * 2 + x_lo), y: 4, z: 8, core: 2. Of those that a mesh axis runs over, the one named last changes fastest.
Arguments:
- checkpoints: bfloat16 [32, 2, 3, 2048, 2048], P('ens', None, None, 'space'), may hold values from -6 to 6
- section_index: int32 [32], P('ens'), may hold values from 0 to 1
- targets: bfloat16 [32, 2048, 2048], P('ens', 'space'), may hold values from -6 to 6
- sea_mask: int32 [2048, 2048], P('space'), may hold values 0 or 1
- basis_rows: bfloat16 [2048, 1024], P('space'), may hold values from -0.5 to 0.5
- basis_cols: bfloat16 [2048, 1024], replicated, may hold values from -0.1875 to 0.1875
- control: float32 [1024, 1024], P('space'), may hold values from -6 to 6
Outputs:
- control_next: float32 [1024, 1024], P('space')
The draws below stay inside these ranges and needn't reach their ends.
Inputs may be any that keep to these rules, and one draw needn't show every extreme that they name: `section_index`: selects one of the 2 slots.
All inputs are finite; a program needn't handle non-finite values. No bound on the sum of `sea_mask` on one device may be relied on, other than what follows from the above.
Results may differ from the reference program's by a relative error of at most 0.0014.
The reference program's roundings to bfloat16 on the way (of `coeffs` and `projected`) count: a program that leaves them out, or rounds other values in their place, can miss the bound.
Values may be sent and summed in bfloat16 or wider, within the bound.
A program may use at most 128 MiB of HBM per device.

```python
import jax
import jax.numpy as jnp
from jax import lax

COLS = 2048
BASIS = 1024
SLOTS = 2
STATES = 32
NX = 2048


def set_ends(result, stream_key, least, high):
    extent = result.shape
    index_at = [jax.random.randint(jax.random.fold_in(stream_key, axis), (), 0, extent[axis]) for axis in range(len(extent))]
    result = result.at[tuple(index_at)].set(least)
    longest = extent.index(max(extent))
    index_at[longest] = (index_at[longest] + 1) % extent[longest]
    return result.at[tuple(index_at)].set(high)


def strengthened(result, own_key, source, target, blocks, factor):
    owner, partner = [(jnp.arange(result.shape[axis_at]) // (result.shape[axis_at] // blocks)).reshape([-1 if axis == axis_at else 1 for axis in range(result.ndim)]) for axis_at in (source, target)]
    chosen = jax.random.permutation(own_key, blocks)[partner]
    strong = (owner == chosen) | (owner == (partner + blocks // 2) % blocks)
    return jnp.where(strong, factor * result, result)


def block_levels(rng, extent, shards, low, largest):
    def one(position, blocks):
        heights = jax.random.uniform(jax.random.fold_in(jax.random.fold_in(rng, 6), position), (blocks,), jnp.float32, low / len(shards), largest / len(shards))
        return jnp.repeat(jnp.exp(heights), extent[position] // blocks).reshape((-1,) + (1,) * (len(extent) - position - 1))

    factor_of = one(*shards[0])
    for cut in shards[1:]:
        factor_of = factor_of * one(*cut)
    return factor_of


def noise(key, dims, width, most, pieces=(), held_as=jnp.bfloat16):
    values = jax.random.normal(key, dims, jnp.float32) * width
    if len(pieces) > 0:
        values = block_levels(key, dims, pieces, -0.22, 0.18) * values
    return jnp.clip(values, min=-most, max=most).astype(held_as)


def noise_with(rng, dims, width, reach, cuts, heavy, kind=jnp.bfloat16):
    values = width * jax.random.normal(rng, dims, jnp.float32)
    if cuts:
        values = values * block_levels(rng, dims, cuts, -0.22, 0.18)
    return jnp.clip(strengthened(values, jax.random.fold_in(rng, 3), *heavy), -reach, reach).astype(kind)


def setup_inputs(seed: int = 0) -> dict:
    arg_keys = jax.random.split(jax.random.key(seed), 8)
    return {
        "checkpoints": noise(arg_keys[0], (STATES, SLOTS, 3, NX, COLS), 1.0, 6.0, ((0, 4), (3, 64))),
        "section_index": set_ends(jax.random.randint(arg_keys[1], (STATES,), 0, SLOTS), jax.random.fold_in(arg_keys[1], 1), 0, SLOTS - 1).astype(jnp.int32),
        "targets": noise(arg_keys[2], (STATES, NX, COLS), 1.0, 6.0, ((0, 4), (1, 64))),
        "sea_mask": set_ends((jax.random.randint(arg_keys[3], (NX, COLS), 0, 4) < 3).astype(jnp.int32), jax.random.fold_in(arg_keys[3], 1), 0, 1),
        "basis_rows": noise_with(arg_keys[4], (NX, BASIS), BASIS ** -0.5, 0.5, ((0, 64),), (0, 1, 64, 4.0)),
        "basis_cols": noise(arg_keys[5], (COLS, BASIS), BASIS ** -0.5, 0.1875),
        "control": noise(arg_keys[6], (BASIS, BASIS), 1.0, 6.0, ((0, 64),), jnp.float32),
    }


DEPTH = 1.0
GRAVITY = 1.0
CORIOLIS = 0.5
FRICTION = 0.1
TIME_STEP = 0.3
STEP_SIZE = 1.0
EPSILON = 1e-06

def across_columns(field):
    widths = [(0, 0)] * (field.ndim - 1) + [(1, 1)]
    padded = jnp.pad(field, widths)
    return 0.5 * (padded[..., 2:] - padded[..., :-2])

def across_rows(field):
    widths = [(0, 0)] * (field.ndim - 2) + [(1, 1), (0, 0)]
    padded = jnp.pad(field, widths)
    return 0.5 * (padded[..., 2:, :] - padded[..., :-2, :])

def height_change(height, east, north):
    return -(across_columns((DEPTH + height) * east) + across_rows((DEPTH + height) * north))

def reference(checkpoints, section_index, targets, sea_mask, basis_rows, basis_cols, control):
    coeffs = jnp.dot(basis_rows, control.astype(jnp.bfloat16), preferred_element_type=jnp.float32).astype(jnp.bfloat16)
    potential = lax.dot_general(coeffs, basis_cols, (((1,), (1,)), ((), ())), preferred_element_type=jnp.float32)
    sea = sea_mask.astype(jnp.float32)

    def one_state(total, item):
        stored, slot, observed = item
        chosen = slot == jnp.arange(SLOTS, dtype=jnp.int32)[:, None, None, None]
        start = lax.optimization_barrier(jnp.sum(jnp.where(chosen, stored, jnp.zeros_like(stored)), axis=0, dtype=jnp.float32))
        observed = observed.astype(jnp.float32)

        def misfit(field):
            stress_x = -across_rows(field)
            stress_y = across_columns(field)
            height_start, east_start, north_start = (start[0], start[1], start[2])
            change_height = height_change(height_start, east_start, north_start)
            change_east = CORIOLIS * north_start - GRAVITY * across_columns(height_start) - FRICTION * east_start + stress_x
            change_north = -CORIOLIS * east_start - GRAVITY * across_rows(height_start) - FRICTION * north_start + stress_y
            height_mid = sea * (height_start + TIME_STEP * change_height)
            east_mid = sea * (east_start + TIME_STEP * change_east)
            north_mid = sea * (north_start + TIME_STEP * change_north)
            change_mid = height_change(height_mid, east_mid, north_mid)
            height_end = sea * (0.5 * height_start + 0.5 * (height_mid + TIME_STEP * change_mid))
            differ = height_end - observed
            return 0.5 * jnp.sum(sea * differ * differ)
        value, pull = jax.vjp(misfit, potential)
        return (total + pull(jnp.ones_like(value))[0], None)
    zeros = jnp.zeros(potential.shape, jnp.float32)
    summed, _ = lax.scan(one_state, zeros, (checkpoints, section_index, targets))
    projected = jnp.dot(summed.astype(jnp.bfloat16), basis_cols, preferred_element_type=jnp.float32).astype(jnp.bfloat16)
    gradient = lax.dot_general(basis_rows, projected, (((0,), (0,)), ((), ())), preferred_element_type=jnp.float32)
    meansq = jnp.mean(gradient * gradient)
    return control - STEP_SIZE * gradient / jnp.sqrt(meansq + EPSILON)
```

```python
import functools

import jax
import jax.numpy as jnp
from jax import lax
from jax.experimental import pallas as pl
from jax.experimental.pallas import tpu as pltpu
from jax.sharding import PartitionSpec as P

MESH = pl.DeviceIdType.MESH
F32 = jnp.float32
BF16 = jnp.bfloat16
EPSILON = 1e-06
LANES = 128
LINE = 8
ENS = 4
YN = 4


def kernel(
    zn,
    si_ref, ck_hbm, tg_hbm, mask_hbm, br_hbm, bc_hbm, ct_hbm, out_ref,
    ck, tg, mk_in, br, bc, ct,
    ctl_s, ctl_g, ext, bhal, hs, hr, hal, mk,
    hm_s, fx_s, fy_s, ab_s, cfs, cfg, pot, px, py, gx, gy,
    gs, gr, ps, pr, g_s, gyr, gy_s, gzr, fs, fr, sys_, syr, szs, szr,
    load_sem, send_sem, recv_sem,
):
    states, rows, cols = ck.shape[0], ck.shape[3], ck.shape[4]
    ring = rows + 8
    nk = cols // LANES
    basis = br.shape[1]
    piece = cols // ENS
    e = lax.axis_index("ens")
    t = lax.axis_index("space")
    x = t // (zn * YN)
    z = (t // YN) % zn
    y = t % YN
    j = x * ENS + e
    count = 2 * zn * YN

    def dev(e2, x2, z2, y2):
        return (e2, (x2 * zn + z2) * YN + y2)

    line = []
    for d in range(1, LINE):
        j2 = (j + d) % LINE
        line.append((j2, dev(j2 % ENS, j2 // ENS, z, y)))
    ys = []
    for d in range(1, YN):
        y2 = (y + d) % YN
        ys.append((y2, dev(e, x, z, y2)))
    zs = []
    for d in range(1, zn):
        z2 = (z + d) % zn
        zs.append((z2, dev(e, x, z2, y)))
    es = []
    for d in range(1, ENS):
        e2 = (e + d) % ENS
        es.append((e2, (e2, t)))
    partner = dev(e, 1 - x, z, y)
    after = (e, (t + 1) % count)
    before = (e, (t + count - 1) % count)

    base = [0]

    def sems(n):
        at = base[0]
        base[0] += n
        return at

    loads = [
        pltpu.make_async_copy(src, dst, load_sem.at[i])
        for i, (src, dst) in enumerate(
            ((ct_hbm, ct), (br_hbm, br), (ck_hbm, ck), (tg_hbm, tg), (mask_hbm, mk_in), (bc_hbm, bc))
        )
    ]
    for load in loads:
        load.start()

    barrier = pltpu.get_barrier_semaphore()
    greet = [d for _, d in line] + [d for _, d in ys] + [d for _, d in zs] + [after, before]
    for d in greet:
        pl.semaphore_signal(barrier, inc=1, device_id=d, device_id_type=MESH)

    def copy(src, dst, at_send, at_recv, device):
        return pltpu.make_async_remote_copy(
            src_ref=src,
            dst_ref=dst,
            send_sem=send_sem.at[at_send],
            recv_sem=recv_sem.at[at_recv],
            device_id=device,
            device_id_type=MESH,
        )

    sent = []

    def exchange(peers, me, n, src_of, dst_of):
        at = sems(n)
        for i, (p, device) in enumerate(peers):
            c = copy(src_of(p), dst_of(me), at + i, at + me, device)
            c.start()
            sent.append(c)

        def wait():
            for p, device in peers:
                copy(src_of(p), dst_of(p), at, at + p, device).wait_recv()

        return wait

    def single(src, dst, device):
        at = sems(1)
        c = copy(src, dst, at, at, device)
        c.start()
        sent.append(c)
        return c.wait_recv

    loads[0].wait()
    for b in range(LINE):
        ctl_s[b] = ct[:, b * LANES : (b + 1) * LANES].astype(BF16)
    ctl_g[x, z, y] = ctl_s[j]
    pl.semaphore_wait(barrier, len(greet))
    a0 = single(ctl_s.at[(1 - x) * ENS + e], ctl_g.at[x, z, y], partner)
    loads[1].wait()
    top_rows = single(br.at[0:16], bhal.at[0], before)
    end_rows = single(br.at[rows - 16 : rows], bhal.at[1], after)
    a0()
    ay = exchange(ys, y, YN, lambda p: ctl_g.at[:, z, y], lambda p: ctl_g.at[:, z, p])

    loads[2].wait()
    loads[3].wait()
    loads[4].wait()
    sub = lax.broadcasted_iota(jnp.int32, (8, cols), 0)

    def tiles(s, field, first):
        slot = si_ref[s]
        block = ck[s, slot, field, first : first + 16, :].astype(F32)
        return block[0:8] if first == 0 else block[8:16]

    last = rows - 16
    for half in range(states // 2):
        up, down = [], []
        for s in (2 * half, 2 * half + 1):
            h, u, v = (tiles(s, f, 0) for f in range(3))
            up.append(jnp.where(sub < 3, h, jnp.where(sub < 6, pltpu.roll(v, 3, 0), pltpu.roll(u, 6, 0))))
            h, u, v = (tiles(s, f, last) for f in range(3))
            down.append(jnp.where(sub >= 5, h, jnp.where(sub >= 2, pltpu.roll(v, 5, 0), pltpu.roll(u, 2, 0))))
        hs[0, half] = jnp.concatenate(up, axis=0).astype(BF16)
        hs[1, half] = jnp.concatenate(down, axis=0).astype(BF16)
    up = jnp.zeros((8, cols), F32)
    down = jnp.zeros((8, cols), F32)
    for s in range(states):
        first = tg[s, 0:16, :].astype(F32)[0:8]
        up = jnp.where(sub == s, first if s == 0 else pltpu.roll(first, s, 0), up)
        final = tg[s, last : last + 16, :].astype(F32)[8:16]
        down = jnp.where(sub == s, final if s == 7 else pltpu.roll(final, s + 1, 0), down)
    hs[0, states // 2] = jnp.concatenate([up, mk_in[0:8, :].astype(F32)], axis=0).astype(BF16)
    hs[1, states // 2] = jnp.concatenate([down, mk_in[rows - 8 : rows, :].astype(F32)], axis=0).astype(BF16)
    from_after = single(hs.at[0], hr.at[0], before)
    from_before = single(hs.at[1], hr.at[1], after)

    ay()
    az = exchange(zs, z, zn, lambda p: ctl_g.at[:, z], lambda p: ctl_g.at[:, p])

    low_end = jnp.where(t < count - 1, 4, 0)
    high_start = jnp.where(t > 0, 4, 8)

    top_rows()
    end_rows()
    subb = lax.broadcasted_iota(jnp.int32, (8, basis), 0)
    edge = jnp.where(
        subb < low_end,
        bhal[0].astype(F32)[0:8],
        jnp.where(subb >= high_start, bhal[1].astype(F32)[8:16], 0.0),
    )
    ext[x, 0:rows] = br[...]
    ext[x, rows : rows + 16] = jnp.concatenate([edge, jnp.zeros_like(edge)], axis=0).astype(BF16)
    other_ext = single(ext.at[x], ext.at[x], partner)

    from_after()
    from_before()

    def joined(low, high):
        return jnp.where(sub < low_end, low, jnp.where(sub >= high_start, high, 0.0))

    for half in range(states // 2):
        low2 = hr[0, half].astype(F32)
        high2 = hr[1, half].astype(F32)
        for i in range(2):
            s = 2 * half + i
            low, high = low2[8 * i : 8 * i + 8], high2[8 * i : 8 * i + 8]
            hal[s, 0] = joined(low, high)
            hal[s, 1] = joined(pltpu.roll(low, 2, 0), pltpu.roll(high, 6, 0))
            hal[s, 2] = joined(pltpu.roll(low, 5, 0), pltpu.roll(high, 3, 0))
    low2 = hr[0, states // 2].astype(F32)
    high2 = hr[1, states // 2].astype(F32)
    for s in range(states):
        low, high = low2[0:8], high2[0:8]
        low = low if s == 0 else pltpu.roll(low, 8 - s, 0)
        high = high if s == 7 else pltpu.roll(high, 7 - s, 0)
        hal[s, 3] = joined(low, high)
    mk[0:rows] = mk_in[...].astype(F32)
    mk[rows:ring] = joined(low2[8:16], high2[8:16])

    az()
    other_ext()
    control_all = ctl_g[...].reshape(basis, LANES)
    lhs = ext[...].reshape(2 * (rows + 16), basis)
    cf = jnp.dot(lhs, control_all, preferred_element_type=F32).astype(BF16)
    cfs[...] = cf.reshape(2, rows + 16, LANES)
    cfg[j] = cfs[x]
    wait_cf = exchange(line, j, LINE, lambda p: cfs.at[p // ENS], lambda p: cfg.at[p])

    lane = lax.broadcasted_iota(jnp.int32, (ring, LANES), 1)
    is_first = lane == 0
    is_last = lane == LANES - 1

    def row_diff(q):
        return pltpu.roll(q, ring - 1, 0) - pltpu.roll(q, 1, 0)

    def turned(q):
        return pltpu.roll(q, LANES - 1, 1), pltpu.roll(q, 1, 1)

    def column_diff(turns, k):
        left = turns[k - 1][1] if k > 0 else 0.0
        right = turns[k + 1][0] if k < nk - 1 else 0.0
        return jnp.where(is_last, right, turns[k][0]) - jnp.where(is_first, left, turns[k][1])

    def at(k):
        return slice(k * LANES, (k + 1) * LANES)

    def before_stress(s, carry):
        slot = si_ref[s]

        def full(field, k):
            own = ck[s, slot, field, :, at(k)].astype(F32)
            return jnp.concatenate([own, hal[s, field, :, at(k)]], axis=0)

        kept, fxt, ht = {}, {}, {}
        for step in range(nk + 1):
            if step < nk:
                k = step
                h, u, v = (full(f, k) for f in range(3))
                g = 1.0 + h
                fx, fy = g * u, g * v
                kept[k] = (h, u, v, row_diff(fy), row_diff(h))
                fxt[k], ht[k] = turned(fx), turned(h)
            if step >= 1:
                k = step - 1
                h, u, v, dyf, dyh = kept.pop(k)
                w = 0.15 * (column_diff(fxt, k) + dyf)
                hm = mk[:, at(k)] * ((1.0 + h) - w)
                ub = 0.97 * u + 0.15 * (v - column_diff(ht, k))
                vb = 0.97 * v - 0.15 * (u + dyh)
                seen = jnp.concatenate([tg[s, :, at(k)].astype(F32), hal[s, 3, :, at(k)]], axis=0)
                hm_s[s, :, at(k)] = hm
                fx_s[s, :, at(k)] = hm * ub
                fy_s[s, :, at(k)] = hm * vb
                ab_s[s, :, at(k)] = 2.0 * (h - seen) - w
        return carry

    lax.fori_loop(0, states, before_stress, 0)

    wait_cf()
    loads[5].wait()
    coeffs = jnp.concatenate([cfg[b] for b in range(LINE)], axis=1)
    pot[...] = lax.dot_general(
        coeffs, bc[...], (((1,), (1,)), ((), ())), preferred_element_type=F32
    )
    turns = {}
    for step in range(nk + 1):
        if step < nk:
            q = pot[0:ring, at(step)]
            turns[step] = turned(q)
            px[:, at(step)] = -0.15 * row_diff(q)
        if step >= 1:
            py[:, at(step - 1)] = 0.15 * column_diff(turns, step - 1)
    gx[...] = jnp.zeros_like(gx)
    gy[...] = jnp.zeros_like(gy)

    def with_stress(s, carry):
        ft, dyf, at_, rows_of, hms = {}, {}, {}, {}, {}
        for step in range(nk + 2):
            if step < nk:
                k = step
                hm = hm_s[s, :, at(k)]
                ft[k] = turned(fx_s[s, :, at(k)] + hm * px[:, at(k)])
                dyf[k] = row_diff(fy_s[s, :, at(k)] + hm * py[:, at(k)])
            if 1 <= step <= nk:
                k = step - 1
                a = mk[:, at(k)] * (ab_s[s, :, at(k)] - 0.15 * (column_diff(ft, k) + dyf.pop(k)))
                at_[k] = turned(a)
                rows_of[k] = row_diff(a)
            if step >= 2:
                k = step - 2
                hm = hm_s[s, :, at(k)]
                gx[:, at(k)] += hm * column_diff(at_, k)
                gy[:, at(k)] += hm * rows_of.pop(k)
        return carry

    lax.fori_loop(0, states, with_stress, 0)

    turns = {}
    per = piece // LANES
    for step in range(nk + 1):
        if step < nk:
            turns[step] = turned(gy[:, at(step)])
        if step >= 1:
            k = step - 1
            value = 0.005625 * (row_diff(gx[:, at(k)]) - column_diff(turns, k))
            gs[k // per, :, at(k % per)] = value[0:rows]

    gr[e] = gs[e]
    exchange(es, e, ENS, lambda p: gs.at[p], lambda p: gr.at[p])()
    summed = ((gr[0] + gr[1]) + (gr[2] + gr[3])).astype(BF16)
    part = jnp.dot(summed, bc[pl.ds(pl.multiple_of(e * piece, piece), piece), :], preferred_element_type=F32)
    for b in range(LINE):
        ps[b] = part[:, b * LANES : (b + 1) * LANES]
    pr[j] = ps[j]
    exchange(line, j, LINE, lambda p: ps.at[p], lambda p: pr.at[p])()
    projected = jnp.concatenate(
        [((pr[0] + pr[1]) + (pr[2] + pr[3])), ((pr[4] + pr[5]) + (pr[6] + pr[7]))], axis=0
    ).astype(BF16)

    rows2 = ext[:, 0:rows, :].reshape(2 * rows, basis)
    g_s[...] = lax.dot_general(
        rows2, projected, (((0,), (0,)), ((), ())), preferred_element_type=F32
    ).reshape(g_s.shape)
    exchange(ys, y, YN, lambda p: g_s.at[:, :, p], lambda p: gyr.at[p])()
    total = g_s[:, :, y]
    for i, (p, _) in enumerate(ys):
        total = total + gyr[p]
    gy_s[...] = total
    exchange(zs, z, zn, lambda p: gy_s.at[:, p], lambda p: gzr.at[p])()
    total = gy_s[:, z]
    for p, _ in zs:
        total = total + gzr[p]

    per_row = total.shape[1]
    squares = total * total
    flat = squares.reshape(2 * per_row // 8, 8, LANES)
    square = flat[0]
    for i in range(1, 2 * per_row // 8):
        square = square + flat[i]
    for b in range(2):
        fs[b, 0:per_row] = total[b]
        fs[b, per_row : per_row + 8] = square
    fr[j] = fs[x]
    exchange(line, j, LINE, lambda p: fs.at[p // ENS], lambda p: fr.at[p])()
    square = fr[0, per_row : per_row + 8]
    for b in range(1, LINE):
        square = square + fr[b, per_row : per_row + 8]
    sys_[...] = square
    syr[y] = square
    exchange(ys, y, YN, lambda p: sys_, lambda p: syr.at[p])()
    square = (syr[0] + syr[1]) + (syr[2] + syr[3])
    szs[...] = square
    szr[z] = square
    exchange(zs, z, zn, lambda p: szs, lambda p: szr.at[p])()
    square = szr[0]
    for b in range(1, zn):
        square = square + szr[b]
    mean = jnp.sum(square, keepdims=True) / (basis * basis)
    root = jnp.sqrt(mean + EPSILON)
    gradient = jnp.concatenate([fr[b, 0:per_row] for b in range(LINE)], axis=1)
    out_ref[...] = ct[...] - gradient / root

    for c in sent:
        c.wait_send()


def on_device(checkpoints, section_index, targets, sea_mask, basis_rows, basis_cols, control):
    states, slots, fields, rows, cols = checkpoints.shape
    basis = basis_cols.shape[1]
    per_row = control.shape[0]
    count = lax.axis_size("space")
    zn = count // (2 * YN)
    ring = rows + 8
    n_sems = 1 + 2 + YN + 2 + zn + 1 + LINE + ENS + LINE + YN + zn + LINE + YN + zn
    any_ = pl.BlockSpec(memory_space=pl.ANY)
    vmem = pltpu.VMEM
    scratch = [
        vmem((states, slots, fields, rows, cols), BF16),
        vmem((states, rows, cols), BF16),
        vmem((rows, cols), jnp.int32),
        vmem((rows, basis), BF16),
        vmem((cols, basis), BF16),
        vmem((per_row, basis), F32),
        vmem((LINE, per_row, LANES), BF16),
        vmem((2, zn, YN, per_row, LANES), BF16),
        vmem((2, rows + 16, basis), BF16),
        vmem((2, 16, basis), BF16),
        vmem((2, states // 2 + 1, 16, cols), BF16),
        vmem((2, states // 2 + 1, 16, cols), BF16),
        vmem((states, 4, 8, cols), F32),
        vmem((ring, cols), F32),
        vmem((states, ring, cols), F32),
        vmem((states, ring, cols), F32),
        vmem((states, ring, cols), F32),
        vmem((states, ring, cols), F32),
        vmem((2, rows + 16, LANES), BF16),
        vmem((LINE, rows + 16, LANES), BF16),
        vmem((rows + 16, cols), F32),
        vmem((ring, cols), F32),
        vmem((ring, cols), F32),
        vmem((ring, cols), F32),
        vmem((ring, cols), F32),
        vmem((ENS, rows, cols // ENS), F32),
        vmem((ENS, rows, cols // ENS), F32),
        vmem((LINE, rows, LANES), F32),
        vmem((LINE, rows, LANES), F32),
        vmem((2, zn, YN, per_row, LANES), F32),
        vmem((YN, 2, zn, per_row, LANES), F32),
        vmem((2, zn, per_row, LANES), F32),
        vmem((zn, 2, per_row, LANES), F32),
        vmem((2, per_row + 8, LANES), F32),
        vmem((LINE, per_row + 8, LANES), F32),
        vmem((8, LANES), F32),
        vmem((YN, 8, LANES), F32),
        vmem((8, LANES), F32),
        vmem((zn, 8, LANES), F32),
        pltpu.SemaphoreType.DMA((6,)),
        pltpu.SemaphoreType.DMA((n_sems,)),
        pltpu.SemaphoreType.DMA((n_sems,)),
    ]
    return pl.pallas_call(
        functools.partial(kernel, zn),
        out_shape=jax.ShapeDtypeStruct(control.shape, F32),
        in_specs=[pl.BlockSpec(memory_space=pltpu.SMEM)] + [any_] * 6,
        out_specs=pl.BlockSpec(memory_space=pltpu.VMEM),
        scratch_shapes=scratch,
        compiler_params=pltpu.CompilerParams(
            collective_id=0, has_side_effects=True, vmem_limit_bytes=60 * 1024 * 1024
        ),
    )(section_index, checkpoints, targets, sea_mask, basis_rows, basis_cols, control)


def solution(mesh):
    return jax.shard_map(
        on_device,
        mesh=mesh,
        in_specs=(
            P("ens", None, None, "space", None),
            P("ens"),
            P("ens", "space", None),
            P("space", None),
            P("space", None),
            P(),
            P("space", None),
        ),
        out_specs=P("space", None),
        check_vma=False,
    )
```

```python
import functools

import jax
import jax.numpy as jnp
from jax import lax
from jax.experimental import pallas as pl
from jax.experimental.pallas import tpu as pltpu
from jax.sharding import PartitionSpec as P

MESH = pl.DeviceIdType.MESH
F32 = jnp.float32
BF16 = jnp.bfloat16
EPSILON = 1e-06
LANES = 128
LINE = 8
ENS = 4
YN = 4
FOLD = 4


def kernel(
    zn,
    si_ref, ck_hbm, tg_hbm, mask_hbm, br_hbm, bc_hbm, ct_hbm, out_ref,
    ck, tg, mk_in, br, bc, ct, bcp, xin,
    ctl_s, ctl_g, ext, bhal, hs, hr, mk, tmp,
    hm_s, fx_s, fy_s, ab_s, cfs, cfg, pot, px, py, gx, gy,
    gs, gr, ps, pr, g_s, gyr, gy_s, gzr, fs, fr, sls, slr, sys_, syr, szs, szr,
    load_sem, send_sem, recv_sem,
):
    states, rows, cols = ck.shape[0], ck.shape[3], ck.shape[4]
    ring = rows + 8
    nk = cols // LANES
    basis = br.shape[1]
    piece = cols // ENS
    e = lax.axis_index("ens")
    t = lax.axis_index("space")
    x = t // (zn * YN)
    z = (t // YN) % zn
    y = t % YN
    j = x * ENS + e
    count = 2 * zn * YN

    def dev(e2, x2, z2, y2):
        return (e2, (x2 * zn + z2) * YN + y2)

    line = []
    for d in range(1, LINE):
        j2 = (j + d) % LINE
        line.append((j2, dev(j2 % ENS, j2 // ENS, z, y)))
    ys = []
    for d in range(1, YN):
        y2 = (y + d) % YN
        ys.append((y2, dev(e, x, z, y2)))
    zs = []
    for d in range(1, zn):
        z2 = (z + d) % zn
        zs.append((z2, dev(e, x, z2, y)))
    xzs = []
    for d in range(1, 2 * zn):
        q2 = (x * zn + z + d) % (2 * zn)
        xzs.append((q2, dev(e, q2 // zn, q2 % zn, y)))
    es = []
    for d in range(1, ENS):
        e2 = (e + d) % ENS
        es.append((e2, (e2, t)))
    partner = dev(e, 1 - x, z, y)
    after = (e, (t + 1) % count)
    before = (e, (t + count - 1) % count)

    base = [0]

    def sems(n):
        at = base[0]
        base[0] += n
        return at

    loads = [
        pltpu.make_async_copy(src, dst, load_sem.at[i])
        for i, (src, dst) in enumerate(
            ((ct_hbm, ct), (br_hbm, br), (ck_hbm, ck), (tg_hbm, tg), (mask_hbm, mk_in), (bc_hbm, bc))
        )
    ]
    for load in loads:
        load.start()

    barrier = pltpu.get_barrier_semaphore()
    greet = [d for _, d in xzs + line + ys] + [after, before]
    for d in greet:
        pl.semaphore_signal(barrier, inc=1, device_id=d, device_id_type=MESH)

    def copy(src, dst, at_send, at_recv, device):
        return pltpu.make_async_remote_copy(
            src_ref=src,
            dst_ref=dst,
            send_sem=send_sem.at[at_send],
            recv_sem=recv_sem.at[at_recv],
            device_id=device,
            device_id_type=MESH,
        )

    sent = []

    def exchange(peers, me, n, src_of, dst_of):
        at = sems(n)
        for i, (p, device) in enumerate(peers):
            c = copy(src_of(p), dst_of(me), at + i, at + me, device)
            c.start()
            sent.append(c)

        def wait():
            for p, device in peers:
                copy(src_of(p), dst_of(p), at, at + p, device).wait_recv()

        return wait

    def single(src, dst, device):
        at = sems(1)
        c = copy(src, dst, at, at, device)
        c.start()
        sent.append(c)
        return c.wait_recv

    loads[0].wait()
    for b in range(LINE):
        ctl_s[b] = ct[:, b * LANES : (b + 1) * LANES].astype(BF16)
    ctl_g[x, z, y] = ctl_s[j]

    loads[2].wait()
    loads[3].wait()
    loads[4].wait()
    sub = lax.broadcasted_iota(jnp.int32, (8, cols), 0)

    def tiles(s, field, first):
        slot = si_ref[s]
        block = ck[s, slot, field, first : first + 16, :].astype(F32)
        return block[0:8] if first == 0 else block[8:16]

    last = rows - 16
    for half in range(states // 2):
        up, down = [], []
        for s in (2 * half, 2 * half + 1):
            h, u, v = (tiles(s, f, 0) for f in range(3))
            up.append(jnp.where(sub < 3, h, jnp.where(sub < 6, pltpu.roll(v, 3, 0), pltpu.roll(u, 6, 0))))
            h, u, v = (tiles(s, f, last) for f in range(3))
            down.append(jnp.where(sub >= 5, h, jnp.where(sub >= 2, pltpu.roll(v, 5, 0), pltpu.roll(u, 2, 0))))
        hs[0, half] = jnp.concatenate(up, axis=0).astype(BF16)
        hs[1, half] = jnp.concatenate(down, axis=0).astype(BF16)
    up = jnp.zeros((8, cols), F32)
    down = jnp.zeros((8, cols), F32)
    for s in range(states):
        first = tg[s, 0:16, :].astype(F32)[0:8]
        up = jnp.where(sub == s, first if s == 0 else pltpu.roll(first, s, 0), up)
        final = tg[s, last : last + 16, :].astype(F32)[8:16]
        down = jnp.where(sub == s, final if s == 7 else pltpu.roll(final, s + 1, 0), down)
    hs[0, states // 2] = jnp.concatenate([up, mk_in[0:8, :].astype(F32)], axis=0).astype(BF16)
    hs[1, states // 2] = jnp.concatenate([down, mk_in[rows - 8 : rows, :].astype(F32)], axis=0).astype(BF16)
    loads[1].wait()

    pl.semaphore_wait(barrier, len(greet))
    axz = exchange(
        xzs, x * zn + z, 2 * zn,
        lambda p: ctl_s.at[(p // zn) * ENS + e],
        lambda p: ctl_g.at[p // zn, p % zn, y],
    )
    top_rows = single(br.at[0:16], bhal.at[0], before)
    end_rows = single(br.at[rows - 16 : rows], bhal.at[1], after)
    from_after = single(hs.at[0], hr.at[0], before)
    from_before = single(hs.at[1], hr.at[1], after)

    wide = FOLD * LANES
    groups = cols // wide
    source = lax.broadcasted_iota(jnp.int32, (wide, wide), 0)
    place = lax.broadcasted_iota(jnp.int32, (wide, wide), 1)
    fold = (source == FOLD * (place % LANES) + place // LANES).astype(F32).astype(BF16)

    def folded(blocks):
        lhs = jnp.concatenate([b[:, g * wide : (g + 1) * wide] for g in range(groups) for b in blocks], axis=0)
        res = jnp.dot(lhs, fold, preferred_element_type=F32)
        high = blocks[0].shape[0]
        n = len(blocks)
        return [
            [res[(g * n + i) * high : (g * n + i + 1) * high] for g in range(groups)] for i in range(n)
        ]

    def own_rows(s, carry):
        slot = si_ref[s]
        parts = folded([ck[s, slot, 0], ck[s, slot, 1], ck[s, slot, 2], tg[s]])
        for i in range(4):
            for g in range(groups):
                xin[s, i, 0:rows, g * wide : (g + 1) * wide] = parts[i][g]
        return carry

    lax.fori_loop(0, states, own_rows, 0)
    (parts,) = folded([mk_in[...].astype(F32).astype(BF16)])
    for g in range(groups):
        mk[0:rows, g * wide : (g + 1) * wide] = parts[g]

    low_end = jnp.where(t < count - 1, 4, 0)
    high_start = jnp.where(t > 0, 4, 8)

    top_rows()
    end_rows()
    subb = lax.broadcasted_iota(jnp.int32, (8, basis), 0)
    edge = jnp.where(
        subb < low_end,
        bhal[0].astype(F32)[0:8],
        jnp.where(subb >= high_start, bhal[1].astype(F32)[8:16], 0.0),
    )
    ext[x, 0:rows] = br[...]
    ext[x, rows : rows + 16] = jnp.concatenate([edge, jnp.zeros_like(edge)], axis=0).astype(BF16)
    other_ext = single(ext.at[x], ext.at[x], partner)

    axz()
    ay = exchange(ys, y, YN, lambda p: ctl_g.at[:, :, y], lambda p: ctl_g.at[:, :, p])

    loads[5].wait()
    fold_t = (place == FOLD * (source % LANES) + source // LANES).astype(F32).astype(BF16)

    def basis_group(g, carry):
        at_g = pl.ds(pl.multiple_of(g * wide, wide), wide)
        bcp[at_g, :] = jnp.dot(fold_t, bc[at_g, :], preferred_element_type=F32).astype(BF16)
        return carry

    lax.fori_loop(0, groups, basis_group, 0)

    from_after()
    from_before()
    subw = lax.broadcasted_iota(jnp.int32, (8, wide), 0)

    def joined(low, high):
        return jnp.where(subw < low_end, low, jnp.where(subw >= high_start, high, 0.0))

    for half in range(states // 2 + 1):
        low4, high4 = folded([hr[0, half], hr[1, half]])
        for g in range(groups):
            at_g = slice(g * wide, (g + 1) * wide)
            low2, high2 = low4[g], high4[g]
            if half < states // 2:
                for i in range(2):
                    s = 2 * half + i
                    low, high = low2[8 * i : 8 * i + 8], high2[8 * i : 8 * i + 8]
                    xin[s, 0, rows:ring, at_g] = joined(low, high)
                    xin[s, 1, rows:ring, at_g] = joined(pltpu.roll(low, 2, 0), pltpu.roll(high, 6, 0))
                    xin[s, 2, rows:ring, at_g] = joined(pltpu.roll(low, 5, 0), pltpu.roll(high, 3, 0))
            else:
                for s in range(states):
                    low, high = low2[0:8], high2[0:8]
                    low = low if s == 0 else pltpu.roll(low, 8 - s, 0)
                    high = high if s == 7 else pltpu.roll(high, 7 - s, 0)
                    xin[s, 3, rows:ring, at_g] = joined(low, high)
                mk[rows:ring, at_g] = joined(low2[8:16], high2[8:16])

    other_ext()
    ay()
    control_all = ctl_g[...].reshape(basis, LANES)
    lhs = ext[...].reshape(2 * (rows + 16), basis)
    cf = jnp.dot(lhs, control_all, preferred_element_type=F32).astype(BF16)
    cfs[...] = cf.reshape(2, rows + 16, LANES)
    cfg[j] = cfs[x]
    wait_cf = exchange(line, j, LINE, lambda p: cfs.at[p // ENS], lambda p: cfg.at[p])

    lane = lax.broadcasted_iota(jnp.int32, (ring, LANES), 1)
    is_first = lane == 0
    is_last = lane == LANES - 1

    def row_diff(q):
        return pltpu.roll(q, ring - 1, 0) - pltpu.roll(q, 1, 0)

    def column_diff(get, k, turned):
        g, p = divmod(k, FOLD)

        def left(c):
            if c not in turned:
                turned[c] = pltpu.roll(get(c), LANES - 1, 1)
            return turned[c]

        def right(c):
            if c not in turned:
                turned[c] = pltpu.roll(get(c), 1, 1)
            return turned[c]

        if p < FOLD - 1:
            plus = get(k + 1)
        else:
            plus = jnp.where(is_last, left(k + 1) if g < groups - 1 else 0.0, left(k - p))
        if p > 0:
            minus = get(k - 1)
        else:
            minus = jnp.where(is_first, right(k - 1) if g > 0 else 0.0, right(k + FOLD - 1))
        return plus - minus

    def at(k):
        return slice(k * LANES, (k + 1) * LANES)

    def chunks(g):
        return range(g * FOLD, (g + 1) * FOLD)

    def before_stress(s, carry):
        fxt, ht = {}, {}
        for step in range(groups + 1):
            if step < groups:
                for k in chunks(step):
                    tmp[0, :, at(k)] = (1.0 + xin[s, 0, :, at(k)]) * xin[s, 1, :, at(k)]
            if step >= 1:
                for k in chunks(step - 1):
                    h, u, v, seen = (xin[s, f, :, at(k)] for f in range(4))
                    g = 1.0 + h
                    w = 0.15 * (column_diff(lambda c: tmp[0, :, at(c)], k, fxt) + row_diff(g * v))
                    hm = mk[:, at(k)] * (g - w)
                    dxh = column_diff(lambda c: xin[s, 0, :, at(c)], k, ht)
                    hm_s[s, :, at(k)] = hm
                    fx_s[s, :, at(k)] = hm * (0.97 * u + 0.15 * (v - dxh))
                    fy_s[s, :, at(k)] = hm * (0.97 * v - 0.15 * (u + row_diff(h)))
                    ab_s[s, :, at(k)] = 2.0 * (h - seen) - w
        return carry

    lax.fori_loop(0, states, before_stress, 0)

    wait_cf()
    coeffs = jnp.concatenate([cfg[b] for b in range(LINE)], axis=1)
    pot[...] = lax.dot_general(
        coeffs, bcp[...], (((1,), (1,)), ((), ())), preferred_element_type=F32
    )
    turns = {}
    for k in range(nk):
        px[:, at(k)] = -0.15 * row_diff(pot[0:ring, at(k)])
        py[:, at(k)] = 0.15 * column_diff(lambda c: pot[0:ring, at(c)], k, turns)
    gx[...] = jnp.zeros_like(gx)
    gy[...] = jnp.zeros_like(gy)

    def with_stress(s, carry):
        ft, at_ = {}, {}
        for step in range(groups + 2):
            if step < groups:
                for k in chunks(step):
                    tmp[0, :, at(k)] = fx_s[s, :, at(k)] + hm_s[s, :, at(k)] * px[:, at(k)]
            if 1 <= step <= groups:
                for k in chunks(step - 1):
                    dyf = row_diff(fy_s[s, :, at(k)] + hm_s[s, :, at(k)] * py[:, at(k)])
                    dxf = column_diff(lambda c: tmp[0, :, at(c)], k, ft)
                    tmp[1, :, at(k)] = mk[:, at(k)] * (ab_s[s, :, at(k)] - 0.15 * (dxf + dyf))
            if step >= 2:
                for k in chunks(step - 2):
                    hm = hm_s[s, :, at(k)]
                    gx[:, at(k)] += hm * column_diff(lambda c: tmp[1, :, at(c)], k, at_)
                    gy[:, at(k)] += hm * row_diff(tmp[1, :, at(k)])
        return carry

    lax.fori_loop(0, states, with_stress, 0)

    turns = {}
    per = piece // LANES
    for k in range(nk):
        dyg = column_diff(lambda c: gy[:, at(c)], k, turns)
        value = 0.005625 * (row_diff(gx[:, at(k)]) - dyg)
        gs[k // per, :, at(k % per)] = value[0:rows]

    gr[e] = gs[e]
    exchange(es, e, ENS, lambda p: gs.at[p], lambda p: gr.at[p])()
    summed = ((gr[0] + gr[1]) + (gr[2] + gr[3])).astype(BF16)
    part = jnp.dot(summed, bcp[pl.ds(pl.multiple_of(e * piece, piece), piece), :], preferred_element_type=F32)
    for b in range(LINE):
        ps[b] = part[:, b * LANES : (b + 1) * LANES]
    pr[j] = ps[j]
    exchange(line, j, LINE, lambda p: ps.at[p], lambda p: pr.at[p])()
    projected = jnp.concatenate(
        [((pr[0] + pr[1]) + (pr[2] + pr[3])), ((pr[4] + pr[5]) + (pr[6] + pr[7]))], axis=0
    ).astype(BF16)

    rows2 = ext[:, 0:rows, :].reshape(2 * rows, basis)
    g_s[...] = lax.dot_general(
        rows2, projected, (((0,), (0,)), ((), ())), preferred_element_type=F32
    ).reshape(g_s.shape)
    order = [zn // 2]
    for d in range(zn // 2 - 1, 0, -1):
        order += [zn // 2 - (zn // 2 - d), zn - d]
    order.append(0)
    arrivals = {}
    for off in order:
        z2 = (z + off) % zn
        arrivals[off] = exchange(
            ys, y, YN,
            lambda p, z2=z2: g_s.at[:, z2, p],
            lambda p, off=off: gyr.at[off, p],
        )
    at_z = sems(zn)
    for i, off in enumerate(order):
        z2 = (z + off) % zn
        arrivals[off]()
        gyr[off, y] = g_s[:, z2, y]
        total = (gyr[off, 0] + gyr[off, 1]) + (gyr[off, 2] + gyr[off, 3])
        if off:
            gy_s[off] = total
            c = copy(gy_s.at[off], gzr.at[z], at_z + i, at_z + z, dev(e, x, z2, y))
            c.start()
            sent.append(c)
        else:
            gzr[z] = total
    for p, device in zs:
        copy(gy_s.at[0], gzr.at[p], at_z, at_z + p, device).wait_recv()
    total = gzr[0]
    for p in range(1, zn):
        total = total + gzr[p]

    per_row = total.shape[1]
    squares = total * total
    flat = squares.reshape(2 * per_row // 8, 8, LANES)
    square = flat[0]
    for i in range(1, 2 * per_row // 8):
        square = square + flat[i]
    sls[...] = square
    slr[j] = square
    line_squares = exchange(line, j, LINE, lambda p: sls, lambda p: slr.at[p])
    fs[...] = total
    fr[j] = fs[x]
    line_rows = exchange(line, j, LINE, lambda p: fs.at[p // ENS], lambda p: fr.at[p])
    line_squares()
    square = slr[0]
    for b in range(1, LINE):
        square = square + slr[b]
    sys_[...] = square
    syr[y] = square
    exchange(ys, y, YN, lambda p: sys_, lambda p: syr.at[p])()
    square = (syr[0] + syr[1]) + (syr[2] + syr[3])
    szs[...] = square
    szr[z] = square
    exchange(zs, z, zn, lambda p: szs, lambda p: szr.at[p])()
    square = szr[0]
    for b in range(1, zn):
        square = square + szr[b]
    mean = jnp.sum(square, keepdims=True) / (basis * basis)
    root = jnp.sqrt(mean + EPSILON)
    line_rows()
    gradient = jnp.concatenate([fr[b] for b in range(LINE)], axis=1)
    out_ref[...] = ct[...] - gradient / root

    for c in sent:
        c.wait_send()


def on_device(checkpoints, section_index, targets, sea_mask, basis_rows, basis_cols, control):
    states, slots, fields, rows, cols = checkpoints.shape
    basis = basis_cols.shape[1]
    per_row = control.shape[0]
    count = lax.axis_size("space")
    zn = count // (2 * YN)
    ring = rows + 8
    n_sems = 2 * zn + 4 + 1 + YN + LINE + ENS + LINE + zn * YN + zn + 2 * LINE + YN + zn
    any_ = pl.BlockSpec(memory_space=pl.ANY)
    vmem = pltpu.VMEM
    scratch = [
        vmem((states, slots, fields, rows, cols), BF16),
        vmem((states, rows, cols), BF16),
        vmem((rows, cols), jnp.int32),
        vmem((rows, basis), BF16),
        vmem((cols, basis), BF16),
        vmem((per_row, basis), F32),
        vmem((cols, basis), BF16),
        vmem((states, 4, ring, cols), F32),
        vmem((LINE, per_row, LANES), BF16),
        vmem((2, zn, YN, per_row, LANES), BF16),
        vmem((2, rows + 16, basis), BF16),
        vmem((2, 16, basis), BF16),
        vmem((2, states // 2 + 1, 16, cols), BF16),
        vmem((2, states // 2 + 1, 16, cols), BF16),
        vmem((ring, cols), F32),
        vmem((2, ring, cols), F32),
        vmem((states, ring, cols), F32),
        vmem((states, ring, cols), F32),
        vmem((states, ring, cols), F32),
        vmem((states, ring, cols), F32),
        vmem((2, rows + 16, LANES), BF16),
        vmem((LINE, rows + 16, LANES), BF16),
        vmem((rows + 16, cols), F32),
        vmem((ring, cols), F32),
        vmem((ring, cols), F32),
        vmem((ring, cols), F32),
        vmem((ring, cols), F32),
        vmem((ENS, rows, cols // ENS), F32),
        vmem((ENS, rows, cols // ENS), F32),
        vmem((LINE, rows, LANES), F32),
        vmem((LINE, rows, LANES), F32),
        vmem((2, zn, YN, per_row, LANES), F32),
        vmem((zn, YN, 2, per_row, LANES), F32),
        vmem((zn, 2, per_row, LANES), F32),
        vmem((zn, 2, per_row, LANES), F32),
        vmem((2, per_row, LANES), F32),
        vmem((LINE, per_row, LANES), F32),
        vmem((8, LANES), F32),
        vmem((LINE, 8, LANES), F32),
        vmem((8, LANES), F32),
        vmem((YN, 8, LANES), F32),
        vmem((8, LANES), F32),
        vmem((zn, 8, LANES), F32),
        pltpu.SemaphoreType.DMA((6,)),
        pltpu.SemaphoreType.DMA((n_sems,)),
        pltpu.SemaphoreType.DMA((n_sems,)),
    ]
    return pl.pallas_call(
        functools.partial(kernel, zn),
        out_shape=jax.ShapeDtypeStruct(control.shape, F32),
        in_specs=[pl.BlockSpec(memory_space=pltpu.SMEM)] + [any_] * 6,
        out_specs=pl.BlockSpec(memory_space=pltpu.VMEM),
        scratch_shapes=scratch,
        compiler_params=pltpu.CompilerParams(
            collective_id=0, has_side_effects=True, vmem_limit_bytes=60 * 1024 * 1024
        ),
    )(section_index, checkpoints, targets, sea_mask, basis_rows, basis_cols, control)


def solution(mesh):
    return jax.shard_map(
        on_device,
        mesh=mesh,
        in_specs=(
            P("ens", None, None, "space", None),
            P("ens"),
            P("ens", "space", None),
            P("space", None),
            P("space", None),
            P(),
            P("space", None),
        ),
        out_specs=P("space", None),
        check_vma=False,
    )
```

```python
import functools

import jax
import jax.numpy as jnp
from jax import lax
from jax.experimental import pallas as pl
from jax.experimental.pallas import tpu as pltpu
from jax.sharding import PartitionSpec as P

MESH = pl.DeviceIdType.MESH
F32 = jnp.float32
BF16 = jnp.bfloat16
EPSILON = 1e-06
LANES = 128
LINE = 8
ENS = 4
YN = 4
EARLY = 2
FOLD = 4


def kernel(
    zn,
    si_ref, ck_hbm, tg_hbm, mask_hbm, br_hbm, bc_hbm, ct_hbm, out_ref,
    ck, tg, mk_in, br, bc, ct, bcp, xin,
    ctl_s, ctl_g, ext, bhal, hs, hr, mk, tmp,
    hm_s, fx_s, fy_s, ab_s, cfs, cfg, pot, px, py, gx, gy,
    gs, gr, ps, pr, g_s, g_n, gyr, gy_s, gzr, fs, fr, sls, slr, sys_, syr, szs, szr,
    load_sem, send_sem, recv_sem,
):
    states, rows, cols = ck.shape[0], ck.shape[3], ck.shape[4]
    ring = rows + 8
    nk = cols // LANES
    basis = br.shape[1]
    piece = cols // ENS
    e = lax.axis_index("ens")
    t = lax.axis_index("space")
    x = t // (zn * YN)
    z = (t // YN) % zn
    y = t % YN
    j = x * ENS + e
    count = 2 * zn * YN

    def dev(e2, x2, z2, y2):
        return (e2, (x2 * zn + z2) * YN + y2)

    line = []
    for d in range(1, LINE):
        j2 = (j + d) % LINE
        line.append((j2, dev(j2 % ENS, j2 // ENS, z, y)))
    ys = []
    for d in range(1, YN):
        y2 = (y + d) % YN
        ys.append((y2, dev(e, x, z, y2)))
    zs = []
    for d in range(1, zn):
        z2 = (z + d) % zn
        zs.append((z2, dev(e, x, z2, y)))
    xzs = []
    for d in range(1, 2 * zn):
        q2 = (x * zn + z + d) % (2 * zn)
        xzs.append((q2, dev(e, q2 // zn, q2 % zn, y)))
    es = []
    for d in range(1, ENS):
        e2 = (e + d) % ENS
        es.append((e2, (e2, t)))
    partner = dev(e, 1 - x, z, y)
    after = (e, (t + 1) % count)
    before = (e, (t + count - 1) % count)

    base = [0]

    def sems(n):
        at = base[0]
        base[0] += n
        return at

    moves = [(ct_hbm, ct), (br_hbm, br)]
    moves += [(ck_hbm.at[i], ck.at[i]) for i in range(states)]
    moves += [(tg_hbm, tg), (mask_hbm, mk_in), (bc_hbm, bc)]
    loads = [pltpu.make_async_copy(src, dst, load_sem.at[i]) for i, (src, dst) in enumerate(moves)]
    for load in loads:
        load.start()
    n_ck = 2

    barrier = pltpu.get_barrier_semaphore()
    greet = [d for _, d in xzs + line + ys] + [after, before]
    for d in greet:
        pl.semaphore_signal(barrier, inc=1, device_id=d, device_id_type=MESH)

    def copy(src, dst, at_send, at_recv, device):
        return pltpu.make_async_remote_copy(
            src_ref=src,
            dst_ref=dst,
            send_sem=send_sem.at[at_send],
            recv_sem=recv_sem.at[at_recv],
            device_id=device,
            device_id_type=MESH,
        )

    sent = []

    def exchange(peers, me, n, src_of, dst_of):
        at = sems(n)
        for i, (p, device) in enumerate(peers):
            c = copy(src_of(p), dst_of(me), at + i, at + me, device)
            c.start()
            sent.append(c)

        def wait():
            for p, device in peers:
                copy(src_of(p), dst_of(p), at, at + p, device).wait_recv()

        return wait

    def single(src, dst, device):
        at = sems(1)
        c = copy(src, dst, at, at, device)
        c.start()
        sent.append(c)
        return c.wait_recv

    loads[0].wait()
    for b in range(LINE):
        ctl_s[b] = ct[:, b * LANES : (b + 1) * LANES].astype(BF16)
    ctl_g[x, z, y] = ctl_s[j]

    pl.semaphore_wait(barrier, len(greet))
    axz = exchange(
        xzs, x * zn + z, 2 * zn,
        lambda p: ctl_s.at[(p // zn) * ENS + e],
        lambda p: ctl_g.at[p // zn, p % zn, y],
    )
    loads[1].wait()
    top_rows = single(br.at[0:16], bhal.at[0], before)
    end_rows = single(br.at[rows - 16 : rows], bhal.at[1], after)

    sub = lax.broadcasted_iota(jnp.int32, (8, cols), 0)

    def tiles(s, field, first):
        at_rows = slice(first, first + 16)
        block = jnp.where(
            si_ref[s] == 0, ck[s, 0, field, at_rows, :].astype(F32), ck[s, 1, field, at_rows, :].astype(F32)
        )
        return block[0:8] if first == 0 else block[8:16]

    last = rows - 16
    edges = []
    for half in range(states // 2):
        if half == EARLY:
            axz()
            ay = exchange(ys, y, YN, lambda p: ctl_g.at[:, :, y], lambda p: ctl_g.at[:, :, p])
        up, down = [], []
        for s in (2 * half, 2 * half + 1):
            loads[n_ck + s].wait()
            h, u, v = (tiles(s, f, 0) for f in range(3))
            up.append(jnp.where(sub < 3, h, jnp.where(sub < 6, pltpu.roll(v, 3, 0), pltpu.roll(u, 6, 0))))
            h, u, v = (tiles(s, f, last) for f in range(3))
            down.append(jnp.where(sub >= 5, h, jnp.where(sub >= 2, pltpu.roll(v, 5, 0), pltpu.roll(u, 2, 0))))
        hs[0, half] = jnp.concatenate(up, axis=0).astype(BF16)
        hs[1, half] = jnp.concatenate(down, axis=0).astype(BF16)
        edges.append(single(hs.at[0, half], hr.at[0, half], before))
        edges.append(single(hs.at[1, half], hr.at[1, half], after))
    loads[n_ck + states].wait()
    loads[n_ck + states + 1].wait()
    up = jnp.zeros((8, cols), F32)
    down = jnp.zeros((8, cols), F32)
    for s in range(states):
        first = tg[s, 0:16, :].astype(F32)[0:8]
        up = jnp.where(sub == s, first if s == 0 else pltpu.roll(first, s, 0), up)
        final = tg[s, last : last + 16, :].astype(F32)[8:16]
        down = jnp.where(sub == s, final if s == 7 else pltpu.roll(final, s + 1, 0), down)
    half = states // 2
    hs[0, half] = jnp.concatenate([up, mk_in[0:8, :].astype(F32)], axis=0).astype(BF16)
    hs[1, half] = jnp.concatenate([down, mk_in[rows - 8 : rows, :].astype(F32)], axis=0).astype(BF16)
    edges.append(single(hs.at[0, half], hr.at[0, half], before))
    edges.append(single(hs.at[1, half], hr.at[1, half], after))

    wide = FOLD * LANES
    groups = cols // wide
    source = lax.broadcasted_iota(jnp.int32, (wide, wide), 0)
    place = lax.broadcasted_iota(jnp.int32, (wide, wide), 1)
    fold = (source == FOLD * (place % LANES) + place // LANES).astype(F32).astype(BF16)

    def folded(blocks):
        lhs = jnp.concatenate([b[:, g * wide : (g + 1) * wide] for g in range(groups) for b in blocks], axis=0)
        res = jnp.dot(lhs, fold, preferred_element_type=F32)
        high = blocks[0].shape[0]
        n = len(blocks)
        return [
            [res[(g * n + i) * high : (g * n + i + 1) * high] for g in range(groups)] for i in range(n)
        ]

    low_end = jnp.where(t < count - 1, 4, 0)
    high_start = jnp.where(t > 0, 4, 8)

    top_rows()
    end_rows()
    subb = lax.broadcasted_iota(jnp.int32, (8, basis), 0)
    edge = jnp.where(
        subb < low_end,
        bhal[0].astype(F32)[0:8],
        jnp.where(subb >= high_start, bhal[1].astype(F32)[8:16], 0.0),
    )
    ext[x, 0:rows] = br[...]
    ext[x, rows : rows + 16] = jnp.concatenate([edge, jnp.zeros_like(edge)], axis=0).astype(BF16)
    other_ext = single(ext.at[x], ext.at[x], partner)

    def own_rows(s, carry):
        slot = si_ref[s]
        parts = folded([ck[s, slot, 0], ck[s, slot, 1], ck[s, slot, 2], tg[s]])
        for i in range(4):
            for g in range(groups):
                xin[s, i, 0:rows, g * wide : (g + 1) * wide] = parts[i][g]
        return carry

    lax.fori_loop(0, states, own_rows, 0)
    (parts,) = folded([mk_in[...].astype(F32).astype(BF16)])
    for g in range(groups):
        mk[0:rows, g * wide : (g + 1) * wide] = parts[g]

    loads[n_ck + states + 2].wait()
    fold_t = (place == FOLD * (source % LANES) + source // LANES).astype(F32).astype(BF16)

    def basis_group(g, carry):
        at_g = pl.ds(pl.multiple_of(g * wide, wide), wide)
        bcp[at_g, :] = jnp.dot(fold_t, bc[at_g, :], preferred_element_type=F32).astype(BF16)
        return carry

    lax.fori_loop(0, groups, basis_group, 0)

    other_ext()
    ay()
    control_all = ctl_g[...].reshape(basis, LANES)
    lhs = ext[...].reshape(2 * (rows + 16), basis)
    cf = jnp.dot(lhs, control_all, preferred_element_type=F32).astype(BF16)
    cfs[...] = cf.reshape(2, rows + 16, LANES)
    cfg[j] = cfs[x]
    wait_cf = exchange(line, j, LINE, lambda p: cfs.at[p // ENS], lambda p: cfg.at[p])

    for wait_edge in edges:
        wait_edge()
    subw = lax.broadcasted_iota(jnp.int32, (8, wide), 0)

    def joined(low, high):
        return jnp.where(subw < low_end, low, jnp.where(subw >= high_start, high, 0.0))

    for half in range(states // 2 + 1):
        low4, high4 = folded([hr[0, half], hr[1, half]])
        for g in range(groups):
            at_g = slice(g * wide, (g + 1) * wide)
            low2, high2 = low4[g], high4[g]
            if half < states // 2:
                for i in range(2):
                    s = 2 * half + i
                    low, high = low2[8 * i : 8 * i + 8], high2[8 * i : 8 * i + 8]
                    xin[s, 0, rows:ring, at_g] = joined(low, high)
                    xin[s, 1, rows:ring, at_g] = joined(pltpu.roll(low, 2, 0), pltpu.roll(high, 6, 0))
                    xin[s, 2, rows:ring, at_g] = joined(pltpu.roll(low, 5, 0), pltpu.roll(high, 3, 0))
            else:
                for s in range(states):
                    low, high = low2[0:8], high2[0:8]
                    low = low if s == 0 else pltpu.roll(low, 8 - s, 0)
                    high = high if s == 7 else pltpu.roll(high, 7 - s, 0)
                    xin[s, 3, rows:ring, at_g] = joined(low, high)
                mk[rows:ring, at_g] = joined(low2[8:16], high2[8:16])

    lane = lax.broadcasted_iota(jnp.int32, (ring, LANES), 1)
    is_first = lane == 0
    is_last = lane == LANES - 1

    def row_diff(q):
        return pltpu.roll(q, ring - 1, 0) - pltpu.roll(q, 1, 0)

    def column_diff(get, k, turned):
        g, p = divmod(k, FOLD)

        def left(c):
            if c not in turned:
                turned[c] = pltpu.roll(get(c), LANES - 1, 1)
            return turned[c]

        def right(c):
            if c not in turned:
                turned[c] = pltpu.roll(get(c), 1, 1)
            return turned[c]

        if p < FOLD - 1:
            plus = get(k + 1)
        else:
            plus = jnp.where(is_last, left(k + 1) if g < groups - 1 else 0.0, left(k - p))
        if p > 0:
            minus = get(k - 1)
        else:
            minus = jnp.where(is_first, right(k - 1) if g > 0 else 0.0, right(k + FOLD - 1))
        return plus - minus

    def at(k):
        return slice(k * LANES, (k + 1) * LANES)

    def chunks(g):
        return range(g * FOLD, (g + 1) * FOLD)

    def before_stress(s, carry):
        fxt, ht = {}, {}
        for step in range(groups + 1):
            if step < groups:
                for k in chunks(step):
                    tmp[0, :, at(k)] = (1.0 + xin[s, 0, :, at(k)]) * xin[s, 1, :, at(k)]
            if step >= 1:
                for k in chunks(step - 1):
                    h, u, v, seen = (xin[s, f, :, at(k)] for f in range(4))
                    g = 1.0 + h
                    w = 0.15 * (column_diff(lambda c: tmp[0, :, at(c)], k, fxt) + row_diff(g * v))
                    hm = mk[:, at(k)] * (g - w)
                    dxh = column_diff(lambda c: xin[s, 0, :, at(c)], k, ht)
                    hm_s[s, :, at(k)] = hm
                    fx_s[s, :, at(k)] = hm * (0.97 * u + 0.15 * (v - dxh))
                    fy_s[s, :, at(k)] = hm * (0.97 * v - 0.15 * (u + row_diff(h)))
                    ab_s[s, :, at(k)] = 2.0 * (h - seen) - w
        return carry

    lax.fori_loop(0, states, before_stress, 0)

    wait_cf()
    coeffs = jnp.concatenate([cfg[b] for b in range(LINE)], axis=1)
    pot[...] = lax.dot_general(
        coeffs, bcp[...], (((1,), (1,)), ((), ())), preferred_element_type=F32
    )
    turns = {}
    for k in range(nk):
        px[:, at(k)] = -0.15 * row_diff(pot[0:ring, at(k)])
        py[:, at(k)] = 0.15 * column_diff(lambda c: pot[0:ring, at(c)], k, turns)
    gx[...] = jnp.zeros_like(gx)
    gy[...] = jnp.zeros_like(gy)

    def with_stress(s, carry):
        ft, at_ = {}, {}
        for step in range(groups + 2):
            if step < groups:
                for k in chunks(step):
                    tmp[0, :, at(k)] = fx_s[s, :, at(k)] + hm_s[s, :, at(k)] * px[:, at(k)]
            if 1 <= step <= groups:
                for k in chunks(step - 1):
                    dyf = row_diff(fy_s[s, :, at(k)] + hm_s[s, :, at(k)] * py[:, at(k)])
                    dxf = column_diff(lambda c: tmp[0, :, at(c)], k, ft)
                    tmp[1, :, at(k)] = mk[:, at(k)] * (ab_s[s, :, at(k)] - 0.15 * (dxf + dyf))
            if step >= 2:
                for k in chunks(step - 2):
                    hm = hm_s[s, :, at(k)]
                    gx[:, at(k)] += hm * column_diff(lambda c: tmp[1, :, at(c)], k, at_)
                    gy[:, at(k)] += hm * row_diff(tmp[1, :, at(k)])
        return carry

    lax.fori_loop(0, states, with_stress, 0)

    turns = {}
    per = piece // LANES
    for k in range(nk):
        dyg = column_diff(lambda c: gy[:, at(c)], k, turns)
        value = 0.005625 * (row_diff(gx[:, at(k)]) - dyg)
        gs[k // per, :, at(k % per)] = value[0:rows]

    gr[e] = gs[e]
    exchange(es, e, ENS, lambda p: gs.at[p], lambda p: gr.at[p])()
    summed = ((gr[0] + gr[1]) + (gr[2] + gr[3])).astype(BF16)
    part = jnp.dot(summed, bcp[pl.ds(pl.multiple_of(e * piece, piece), piece), :], preferred_element_type=F32)
    for b in range(LINE):
        ps[b] = part[:, b * LANES : (b + 1) * LANES]
    pr[j] = ps[j]
    exchange(line, j, LINE, lambda p: ps.at[p], lambda p: pr.at[p])()
    projected = jnp.concatenate(
        [((pr[0] + pr[1]) + (pr[2] + pr[3])), ((pr[4] + pr[5]) + (pr[6] + pr[7]))], axis=0
    ).astype(BF16)

    rows2 = ext[:, 0:rows, :].reshape(2 * rows, basis)
    g_s[...] = lax.dot_general(
        rows2, projected, (((0,), (0,)), ((), ())), preferred_element_type=F32
    ).reshape(g_s.shape)
    g_n[...] = g_s[...].astype(BF16)
    order = [zn // 2]
    for d in range(zn // 2 - 1, 0, -1):
        order += [zn // 2 - (zn // 2 - d), zn - d]
    order.append(0)
    arrivals = {}
    for off in order:
        z2 = (z + off) % zn
        arrivals[off] = exchange(
            ys, y, YN,
            lambda p, z2=z2: g_n.at[:, z2, p],
            lambda p, off=off: gyr.at[off, p],
        )
    at_z = sems(zn)
    for i, off in enumerate(order):
        z2 = (z + off) % zn
        arrivals[off]()
        total = g_s[:, z2, y]
        for p, _ in ys:
            total = total + gyr[off, p].astype(F32)
        if off:
            gy_s[off] = total
            c = copy(gy_s.at[off], gzr.at[z], at_z + i, at_z + z, dev(e, x, z2, y))
            c.start()
            sent.append(c)
        else:
            gzr[z] = total
    for p, device in zs:
        copy(gy_s.at[0], gzr.at[p], at_z, at_z + p, device).wait_recv()
    total = gzr[0]
    for p in range(1, zn):
        total = total + gzr[p]

    per_row = total.shape[1]
    squares = total * total
    flat = squares.reshape(2 * per_row // 8, 8, LANES)
    square = flat[0]
    for i in range(1, 2 * per_row // 8):
        square = square + flat[i]
    sls[...] = square
    slr[j] = square
    line_squares = exchange(line, j, LINE, lambda p: sls, lambda p: slr.at[p])
    fs[...] = total
    fr[j] = fs[x]
    line_rows = exchange(line, j, LINE, lambda p: fs.at[p // ENS], lambda p: fr.at[p])
    line_squares()
    square = slr[0]
    for b in range(1, LINE):
        square = square + slr[b]
    sys_[...] = square
    syr[y] = square
    exchange(ys, y, YN, lambda p: sys_, lambda p: syr.at[p])()
    square = (syr[0] + syr[1]) + (syr[2] + syr[3])
    szs[...] = square
    szr[z] = square
    exchange(zs, z, zn, lambda p: szs, lambda p: szr.at[p])()
    square = szr[0]
    for b in range(1, zn):
        square = square + szr[b]
    mean = jnp.sum(square, keepdims=True) / (basis * basis)
    root = jnp.sqrt(mean + EPSILON)
    line_rows()
    gradient = jnp.concatenate([fr[b] for b in range(LINE)], axis=1)
    out_ref[...] = ct[...] - gradient / root

    for c in sent:
        c.wait_send()


def on_device(checkpoints, section_index, targets, sea_mask, basis_rows, basis_cols, control):
    states, slots, fields, rows, cols = checkpoints.shape
    basis = basis_cols.shape[1]
    per_row = control.shape[0]
    count = lax.axis_size("space")
    zn = count // (2 * YN)
    ring = rows + 8
    n_sems = 2 * zn + 2 + 2 * (states // 2 + 1) + 1 + YN + LINE + ENS + LINE + zn * YN + zn + 2 * LINE + YN + zn
    any_ = pl.BlockSpec(memory_space=pl.ANY)
    vmem = pltpu.VMEM
    scratch = [
        vmem((states, slots, fields, rows, cols), BF16),
        vmem((states, rows, cols), BF16),
        vmem((rows, cols), jnp.int32),
        vmem((rows, basis), BF16),
        vmem((cols, basis), BF16),
        vmem((per_row, basis), F32),
        vmem((cols, basis), BF16),
        vmem((states, 4, ring, cols), F32),
        vmem((LINE, per_row, LANES), BF16),
        vmem((2, zn, YN, per_row, LANES), BF16),
        vmem((2, rows + 16, basis), BF16),
        vmem((2, 16, basis), BF16),
        vmem((2, states // 2 + 1, 16, cols), BF16),
        vmem((2, states // 2 + 1, 16, cols), BF16),
        vmem((ring, cols), F32),
        vmem((2, ring, cols), F32),
        vmem((states, ring, cols), F32),
        vmem((states, ring, cols), F32),
        vmem((states, ring, cols), F32),
        vmem((states, ring, cols), F32),
        vmem((2, rows + 16, LANES), BF16),
        vmem((LINE, rows + 16, LANES), BF16),
        vmem((rows + 16, cols), F32),
        vmem((ring, cols), F32),
        vmem((ring, cols), F32),
        vmem((ring, cols), F32),
        vmem((ring, cols), F32),
        vmem((ENS, rows, cols // ENS), F32),
        vmem((ENS, rows, cols // ENS), F32),
        vmem((LINE, rows, LANES), F32),
        vmem((LINE, rows, LANES), F32),
        vmem((2, zn, YN, per_row, LANES), F32),
        vmem((2, zn, YN, per_row, LANES), BF16),
        vmem((zn, YN, 2, per_row, LANES), BF16),
        vmem((zn, 2, per_row, LANES), F32),
        vmem((zn, 2, per_row, LANES), F32),
        vmem((2, per_row, LANES), F32),
        vmem((LINE, per_row, LANES), F32),
        vmem((8, LANES), F32),
        vmem((LINE, 8, LANES), F32),
        vmem((8, LANES), F32),
        vmem((YN, 8, LANES), F32),
        vmem((8, LANES), F32),
        vmem((zn, 8, LANES), F32),
        pltpu.SemaphoreType.DMA((states + 5,)),
        pltpu.SemaphoreType.DMA((n_sems,)),
        pltpu.SemaphoreType.DMA((n_sems,)),
    ]
    return pl.pallas_call(
        functools.partial(kernel, zn),
        out_shape=jax.ShapeDtypeStruct(control.shape, F32),
        in_specs=[pl.BlockSpec(memory_space=pltpu.SMEM)] + [any_] * 6,
        out_specs=pl.BlockSpec(memory_space=pltpu.VMEM),
        scratch_shapes=scratch,
        compiler_params=pltpu.CompilerParams(
            collective_id=0, has_side_effects=True, vmem_limit_bytes=60 * 1024 * 1024
        ),
    )(section_index, checkpoints, targets, sea_mask, basis_rows, basis_cols, control)


def solution(mesh):
    return jax.shard_map(
        on_device,
        mesh=mesh,
        in_specs=(
            P("ens", None, None, "space", None),
            P("ens"),
            P("ens", "space", None),
            P("space", None),
            P("space", None),
            P(),
            P("space", None),
        ),
        out_specs=P("space", None),
        check_vma=False,
    )
```

```python
import functools

import jax
import jax.numpy as jnp
from jax import lax
from jax.experimental import pallas as pl
from jax.experimental.pallas import tpu as pltpu
from jax.sharding import PartitionSpec as P

MESH = pl.DeviceIdType.MESH
F32 = jnp.float32
BF16 = jnp.bfloat16
EPSILON = 1e-06
LANES = 128
LINE = 8
ENS = 4
YN = 4
EARLY = 2
FOLD = 4


def kernel(
    zn,
    si_ref, ck_hbm, tg_hbm, mask_hbm, br_hbm, bc_hbm, ct_hbm, out_ref,
    ck, tg, mk_in, br, bc, ct, bcp, xin,
    ctl_s, ctl_g, ext, bhal, hs, hr, mk, tmp,
    hm_s, fx_s, fy_s, ab_s, cfs, cfg, pot, px, py, gx, gy,
    gs, gr, ps, pr, g_s, g_n, gfr, gyr, gy_s, gzr, fs, fr, sls, slr, sys_, syr, szs, szr,
    load_sem, send_sem, recv_sem,
):
    states, rows, cols = ck.shape[0], ck.shape[3], ck.shape[4]
    ring = rows + 8
    nk = cols // LANES
    basis = br.shape[1]
    piece = cols // ENS
    e = lax.axis_index("ens")
    t = lax.axis_index("space")
    x = t // (zn * YN)
    z = (t // YN) % zn
    y = t % YN
    j = x * ENS + e
    count = 2 * zn * YN

    def dev(e2, x2, z2, y2):
        return (e2, (x2 * zn + z2) * YN + y2)

    line = []
    for d in range(1, LINE):
        j2 = (j + d) % LINE
        line.append((j2, dev(j2 % ENS, j2 // ENS, z, y)))
    ys = []
    for d in range(1, YN):
        y2 = (y + d) % YN
        ys.append((y2, dev(e, x, z, y2)))
    zs = []
    for d in range(1, zn):
        z2 = (z + d) % zn
        zs.append((z2, dev(e, x, z2, y)))
    xzs = []
    for d in range(1, 2 * zn):
        q2 = (x * zn + z + d) % (2 * zn)
        xzs.append((q2, dev(e, q2 // zn, q2 % zn, y)))
    es = []
    for d in range(1, ENS):
        e2 = (e + d) % ENS
        es.append((e2, (e2, t)))
    partner = dev(e, 1 - x, z, y)
    after = (e, (t + 1) % count)
    before = (e, (t + count - 1) % count)

    base = [0]

    def sems(n):
        at = base[0]
        base[0] += n
        return at

    moves = [(ct_hbm, ct), (br_hbm, br)]
    moves += [(ck_hbm.at[i], ck.at[i]) for i in range(states)]
    moves += [(tg_hbm, tg), (mask_hbm, mk_in), (bc_hbm, bc)]
    loads = [pltpu.make_async_copy(src, dst, load_sem.at[i]) for i, (src, dst) in enumerate(moves)]
    for load in loads:
        load.start()
    n_ck = 2

    barrier = pltpu.get_barrier_semaphore()
    greet = [d for _, d in xzs + line + ys] + [after, before]
    for d in greet:
        pl.semaphore_signal(barrier, inc=1, device_id=d, device_id_type=MESH)

    def copy(src, dst, at_send, at_recv, device):
        return pltpu.make_async_remote_copy(
            src_ref=src,
            dst_ref=dst,
            send_sem=send_sem.at[at_send],
            recv_sem=recv_sem.at[at_recv],
            device_id=device,
            device_id_type=MESH,
        )

    sent = []

    def exchange(peers, me, n, src_of, dst_of):
        at = sems(n)
        for i, (p, device) in enumerate(peers):
            c = copy(src_of(p), dst_of(me), at + i, at + me, device)
            c.start()
            sent.append(c)

        def wait():
            for p, device in peers:
                copy(src_of(p), dst_of(p), at, at + p, device).wait_recv()

        return wait

    def single(src, dst, device):
        at = sems(1)
        c = copy(src, dst, at, at, device)
        c.start()
        sent.append(c)
        return c.wait_recv

    loads[0].wait()
    for b in range(LINE):
        ctl_s[b] = ct[:, b * LANES : (b + 1) * LANES].astype(BF16)
    ctl_g[x, z, y] = ctl_s[j]

    pl.semaphore_wait(barrier, len(greet))
    axz = exchange(
        xzs, x * zn + z, 2 * zn,
        lambda p: ctl_s.at[(p // zn) * ENS + e],
        lambda p: ctl_g.at[p // zn, p % zn, y],
    )
    loads[1].wait()
    top_rows = single(br.at[0:16], bhal.at[0], before)
    end_rows = single(br.at[rows - 16 : rows], bhal.at[1], after)

    sub = lax.broadcasted_iota(jnp.int32, (8, cols), 0)

    def tiles(s, field, first):
        at_rows = slice(first, first + 16)
        block = jnp.where(
            si_ref[s] == 0, ck[s, 0, field, at_rows, :].astype(F32), ck[s, 1, field, at_rows, :].astype(F32)
        )
        return block[0:8] if first == 0 else block[8:16]

    last = rows - 16
    edges = []
    for half in range(states // 2):
        if half == EARLY:
            axz()
            ay = exchange(ys, y, YN, lambda p: ctl_g.at[:, :, y], lambda p: ctl_g.at[:, :, p])
        up, down = [], []
        for s in (2 * half, 2 * half + 1):
            loads[n_ck + s].wait()
            h, u, v = (tiles(s, f, 0) for f in range(3))
            up.append(jnp.where(sub < 3, h, jnp.where(sub < 6, pltpu.roll(v, 3, 0), pltpu.roll(u, 6, 0))))
            h, u, v = (tiles(s, f, last) for f in range(3))
            down.append(jnp.where(sub >= 5, h, jnp.where(sub >= 2, pltpu.roll(v, 5, 0), pltpu.roll(u, 2, 0))))
        hs[0, half] = jnp.concatenate(up, axis=0).astype(BF16)
        hs[1, half] = jnp.concatenate(down, axis=0).astype(BF16)
        edges.append(single(hs.at[0, half], hr.at[0, half], before))
        edges.append(single(hs.at[1, half], hr.at[1, half], after))
    loads[n_ck + states].wait()
    loads[n_ck + states + 1].wait()
    up = jnp.zeros((8, cols), F32)
    down = jnp.zeros((8, cols), F32)
    for s in range(states):
        first = tg[s, 0:16, :].astype(F32)[0:8]
        up = jnp.where(sub == s, first if s == 0 else pltpu.roll(first, s, 0), up)
        final = tg[s, last : last + 16, :].astype(F32)[8:16]
        down = jnp.where(sub == s, final if s == 7 else pltpu.roll(final, s + 1, 0), down)
    half = states // 2
    hs[0, half] = jnp.concatenate([up, mk_in[0:8, :].astype(F32)], axis=0).astype(BF16)
    hs[1, half] = jnp.concatenate([down, mk_in[rows - 8 : rows, :].astype(F32)], axis=0).astype(BF16)
    edges.append(single(hs.at[0, half], hr.at[0, half], before))
    edges.append(single(hs.at[1, half], hr.at[1, half], after))

    wide = FOLD * LANES
    groups = cols // wide
    source = lax.broadcasted_iota(jnp.int32, (wide, wide), 0)
    place = lax.broadcasted_iota(jnp.int32, (wide, wide), 1)
    fold = (source == FOLD * (place % LANES) + place // LANES).astype(F32).astype(BF16)

    def folded(blocks):
        lhs = jnp.concatenate([b[:, g * wide : (g + 1) * wide] for g in range(groups) for b in blocks], axis=0)
        res = jnp.dot(lhs, fold, preferred_element_type=F32)
        high = blocks[0].shape[0]
        n = len(blocks)
        return [
            [res[(g * n + i) * high : (g * n + i + 1) * high] for g in range(groups)] for i in range(n)
        ]

    low_end = jnp.where(t < count - 1, 4, 0)
    high_start = jnp.where(t > 0, 4, 8)

    top_rows()
    end_rows()
    subb = lax.broadcasted_iota(jnp.int32, (8, basis), 0)
    edge = jnp.where(
        subb < low_end,
        bhal[0].astype(F32)[0:8],
        jnp.where(subb >= high_start, bhal[1].astype(F32)[8:16], 0.0),
    )
    ext[x, 0:rows] = br[...]
    ext[x, rows : rows + 16] = jnp.concatenate([edge, jnp.zeros_like(edge)], axis=0).astype(BF16)
    other_ext = single(ext.at[x], ext.at[x], partner)

    def own_rows(s, carry):
        slot = si_ref[s]
        parts = folded([ck[s, slot, 0], ck[s, slot, 1], ck[s, slot, 2], tg[s]])
        for i in range(4):
            for g in range(groups):
                xin[s, i, 0:rows, g * wide : (g + 1) * wide] = parts[i][g]
        return carry

    lax.fori_loop(0, states, own_rows, 0)
    (parts,) = folded([mk_in[...].astype(F32).astype(BF16)])
    for g in range(groups):
        mk[0:rows, g * wide : (g + 1) * wide] = parts[g]

    loads[n_ck + states + 2].wait()
    fold_t = (place == FOLD * (source % LANES) + source // LANES).astype(F32).astype(BF16)

    def basis_group(g, carry):
        at_g = pl.ds(pl.multiple_of(g * wide, wide), wide)
        bcp[at_g, :] = jnp.dot(fold_t, bc[at_g, :], preferred_element_type=F32).astype(BF16)
        return carry

    lax.fori_loop(0, groups, basis_group, 0)

    other_ext()
    ay()
    control_all = ctl_g[...].reshape(basis, LANES)
    lhs = ext[...].reshape(2 * (rows + 16), basis)
    cf = jnp.dot(lhs, control_all, preferred_element_type=F32).astype(BF16)
    cfs[...] = cf.reshape(2, rows + 16, LANES)
    cfg[j] = cfs[x]
    wait_cf = exchange(line, j, LINE, lambda p: cfs.at[p // ENS], lambda p: cfg.at[p])

    for wait_edge in edges:
        wait_edge()
    subw = lax.broadcasted_iota(jnp.int32, (8, wide), 0)

    def joined(low, high):
        return jnp.where(subw < low_end, low, jnp.where(subw >= high_start, high, 0.0))

    for half in range(states // 2 + 1):
        low4, high4 = folded([hr[0, half], hr[1, half]])
        for g in range(groups):
            at_g = slice(g * wide, (g + 1) * wide)
            low2, high2 = low4[g], high4[g]
            if half < states // 2:
                for i in range(2):
                    s = 2 * half + i
                    low, high = low2[8 * i : 8 * i + 8], high2[8 * i : 8 * i + 8]
                    xin[s, 0, rows:ring, at_g] = joined(low, high)
                    xin[s, 1, rows:ring, at_g] = joined(pltpu.roll(low, 2, 0), pltpu.roll(high, 6, 0))
                    xin[s, 2, rows:ring, at_g] = joined(pltpu.roll(low, 5, 0), pltpu.roll(high, 3, 0))
            else:
                for s in range(states):
                    low, high = low2[0:8], high2[0:8]
                    low = low if s == 0 else pltpu.roll(low, 8 - s, 0)
                    high = high if s == 7 else pltpu.roll(high, 7 - s, 0)
                    xin[s, 3, rows:ring, at_g] = joined(low, high)
                mk[rows:ring, at_g] = joined(low2[8:16], high2[8:16])

    lane = lax.broadcasted_iota(jnp.int32, (ring, LANES), 1)
    is_first = lane == 0
    is_last = lane == LANES - 1

    def row_diff(q):
        return pltpu.roll(q, ring - 1, 0) - pltpu.roll(q, 1, 0)

    def column_diff(get, k, turned):
        g, p = divmod(k, FOLD)

        def left(c):
            if c not in turned:
                turned[c] = pltpu.roll(get(c), LANES - 1, 1)
            return turned[c]

        def right(c):
            if c not in turned:
                turned[c] = pltpu.roll(get(c), 1, 1)
            return turned[c]

        if p < FOLD - 1:
            plus = get(k + 1)
        else:
            plus = jnp.where(is_last, left(k + 1) if g < groups - 1 else 0.0, left(k - p))
        if p > 0:
            minus = get(k - 1)
        else:
            minus = jnp.where(is_first, right(k - 1) if g > 0 else 0.0, right(k + FOLD - 1))
        return plus - minus

    def at(k):
        return slice(k * LANES, (k + 1) * LANES)

    def chunks(g):
        return range(g * FOLD, (g + 1) * FOLD)

    def before_stress(s, carry):
        fxt, ht = {}, {}
        for step in range(groups + 1):
            if step < groups:
                for k in chunks(step):
                    tmp[0, :, at(k)] = (1.0 + xin[s, 0, :, at(k)]) * xin[s, 1, :, at(k)]
            if step >= 1:
                for k in chunks(step - 1):
                    h, u, v, seen = (xin[s, f, :, at(k)] for f in range(4))
                    g = 1.0 + h
                    w = 0.15 * (column_diff(lambda c: tmp[0, :, at(c)], k, fxt) + row_diff(g * v))
                    hm = mk[:, at(k)] * (g - w)
                    dxh = column_diff(lambda c: xin[s, 0, :, at(c)], k, ht)
                    hm_s[s, :, at(k)] = hm
                    fx_s[s, :, at(k)] = hm * (0.97 * u + 0.15 * (v - dxh))
                    fy_s[s, :, at(k)] = hm * (0.97 * v - 0.15 * (u + row_diff(h)))
                    ab_s[s, :, at(k)] = 2.0 * (h - seen) - w
        return carry

    lax.fori_loop(0, states, before_stress, 0)

    wait_cf()
    coeffs = jnp.concatenate([cfg[b] for b in range(LINE)], axis=1)
    pot[...] = lax.dot_general(
        coeffs, bcp[...], (((1,), (1,)), ((), ())), preferred_element_type=F32
    )
    turns = {}
    for k in range(nk):
        px[:, at(k)] = -0.15 * row_diff(pot[0:ring, at(k)])
        py[:, at(k)] = 0.15 * column_diff(lambda c: pot[0:ring, at(c)], k, turns)
    gx[...] = jnp.zeros_like(gx)
    gy[...] = jnp.zeros_like(gy)

    def with_stress(s, carry):
        ft, at_ = {}, {}
        for step in range(groups + 2):
            if step < groups:
                for k in chunks(step):
                    tmp[0, :, at(k)] = fx_s[s, :, at(k)] + hm_s[s, :, at(k)] * px[:, at(k)]
            if 1 <= step <= groups:
                for k in chunks(step - 1):
                    dyf = row_diff(fy_s[s, :, at(k)] + hm_s[s, :, at(k)] * py[:, at(k)])
                    dxf = column_diff(lambda c: tmp[0, :, at(c)], k, ft)
                    tmp[1, :, at(k)] = mk[:, at(k)] * (ab_s[s, :, at(k)] - 0.15 * (dxf + dyf))
            if step >= 2:
                for k in chunks(step - 2):
                    hm = hm_s[s, :, at(k)]
                    gx[:, at(k)] += hm * column_diff(lambda c: tmp[1, :, at(c)], k, at_)
                    gy[:, at(k)] += hm * row_diff(tmp[1, :, at(k)])
        return carry

    lax.fori_loop(0, states, with_stress, 0)

    turns = {}
    per = piece // LANES
    for k in range(nk):
        dyg = column_diff(lambda c: gy[:, at(c)], k, turns)
        value = 0.005625 * (row_diff(gx[:, at(k)]) - dyg)
        gs[k // per, :, at(k % per)] = value[0:rows]

    gr[e] = gs[e]
    exchange(es, e, ENS, lambda p: gs.at[p], lambda p: gr.at[p])()
    summed = ((gr[0] + gr[1]) + (gr[2] + gr[3])).astype(BF16)
    part = jnp.dot(summed, bcp[pl.ds(pl.multiple_of(e * piece, piece), piece), :], preferred_element_type=F32)
    for b in range(LINE):
        ps[b] = part[:, b * LANES : (b + 1) * LANES]
    pr[j] = ps[j]
    exchange(line, j, LINE, lambda p: ps.at[p], lambda p: pr.at[p])()
    projected = jnp.concatenate(
        [((pr[0] + pr[1]) + (pr[2] + pr[3])), ((pr[4] + pr[5]) + (pr[6] + pr[7]))], axis=0
    ).astype(BF16)

    rows2 = ext[:, 0:rows, :].reshape(2 * rows, basis)
    g_s[...] = lax.dot_general(
        rows2, projected, (((0,), (0,)), ((), ())), preferred_element_type=F32
    ).reshape(g_s.shape)
    g_n[...] = g_s[:, :, ys[1][0]].astype(BF16)
    order = [zn // 2]
    for d in range(zn // 2 - 1, 0, -1):
        order += [zn // 2 - (zn // 2 - d), zn - d]
    order.append(0)
    arrivals = {}
    for off in order:
        z2 = (z + off) % zn
        far = single(g_n.at[:, z2], gfr.at[off], ys[1][1])
        near = exchange(
            (ys[0], ys[2]), y, YN,
            lambda p, z2=z2: g_s.at[:, z2, p],
            lambda p, off=off: gyr.at[off, p],
        )
        arrivals[off] = (far, near)
    at_z = sems(zn)
    for i, off in enumerate(order):
        z2 = (z + off) % zn
        for wait in arrivals[off]:
            wait()
        total = (gyr[off, ys[0][0]] + gyr[off, ys[2][0]]) + (g_s[:, z2, y] + gfr[off].astype(F32))
        if off:
            gy_s[off] = total
            c = copy(gy_s.at[off], gzr.at[z], at_z + i, at_z + z, dev(e, x, z2, y))
            c.start()
            sent.append(c)
        else:
            gzr[z] = total
    for p, device in zs:
        copy(gy_s.at[0], gzr.at[p], at_z, at_z + p, device).wait_recv()
    total = gzr[0]
    for p in range(1, zn):
        total = total + gzr[p]

    per_row = total.shape[1]
    squares = total * total
    flat = squares.reshape(2 * per_row // 8, 8, LANES)
    square = flat[0]
    for i in range(1, 2 * per_row // 8):
        square = square + flat[i]
    sls[...] = square
    slr[j] = square
    line_squares = exchange(line, j, LINE, lambda p: sls, lambda p: slr.at[p])
    fs[...] = total
    fr[j] = fs[x]
    line_rows = exchange(line, j, LINE, lambda p: fs.at[p // ENS], lambda p: fr.at[p])
    line_squares()
    square = slr[0]
    for b in range(1, LINE):
        square = square + slr[b]
    sys_[...] = square
    syr[y] = square
    exchange(ys, y, YN, lambda p: sys_, lambda p: syr.at[p])()
    square = (syr[0] + syr[1]) + (syr[2] + syr[3])
    szs[...] = square
    szr[z] = square
    early = list(sent)
    wait_squares = exchange(zs, z, zn, lambda p: szs, lambda p: szr.at[p])
    line_rows()
    gradient = jnp.concatenate([fr[b] for b in range(LINE)], axis=1)
    for c in early:
        c.wait_send()
    wait_squares()
    square = szr[0]
    for b in range(1, zn):
        square = square + szr[b]
    mean = jnp.sum(square, keepdims=True) / (basis * basis)
    root = jnp.sqrt(mean + EPSILON)
    out_ref[...] = ct[...] - gradient / root

    for c in sent[len(early) :]:
        c.wait_send()


def on_device(checkpoints, section_index, targets, sea_mask, basis_rows, basis_cols, control):
    states, slots, fields, rows, cols = checkpoints.shape
    basis = basis_cols.shape[1]
    per_row = control.shape[0]
    count = lax.axis_size("space")
    zn = count // (2 * YN)
    ring = rows + 8
    n_sems = 2 * zn + 2 + 2 * (states // 2 + 1) + 1 + YN + LINE + ENS + LINE + zn * (YN + 1) + zn + 2 * LINE + YN + zn
    any_ = pl.BlockSpec(memory_space=pl.ANY)
    vmem = pltpu.VMEM
    scratch = [
        vmem((states, slots, fields, rows, cols), BF16),
        vmem((states, rows, cols), BF16),
        vmem((rows, cols), jnp.int32),
        vmem((rows, basis), BF16),
        vmem((cols, basis), BF16),
        vmem((per_row, basis), F32),
        vmem((cols, basis), BF16),
        vmem((states, 4, ring, cols), F32),
        vmem((LINE, per_row, LANES), BF16),
        vmem((2, zn, YN, per_row, LANES), BF16),
        vmem((2, rows + 16, basis), BF16),
        vmem((2, 16, basis), BF16),
        vmem((2, states // 2 + 1, 16, cols), BF16),
        vmem((2, states // 2 + 1, 16, cols), BF16),
        vmem((ring, cols), F32),
        vmem((2, ring, cols), F32),
        vmem((states, ring, cols), F32),
        vmem((states, ring, cols), F32),
        vmem((states, ring, cols), F32),
        vmem((states, ring, cols), F32),
        vmem((2, rows + 16, LANES), BF16),
        vmem((LINE, rows + 16, LANES), BF16),
        vmem((rows + 16, cols), F32),
        vmem((ring, cols), F32),
        vmem((ring, cols), F32),
        vmem((ring, cols), F32),
        vmem((ring, cols), F32),
        vmem((ENS, rows, cols // ENS), F32),
        vmem((ENS, rows, cols // ENS), F32),
        vmem((LINE, rows, LANES), F32),
        vmem((LINE, rows, LANES), F32),
        vmem((2, zn, YN, per_row, LANES), F32),
        vmem((2, zn, per_row, LANES), BF16),
        vmem((zn, 2, per_row, LANES), BF16),
        vmem((zn, YN, 2, per_row, LANES), F32),
        vmem((zn, 2, per_row, LANES), F32),
        vmem((zn, 2, per_row, LANES), F32),
        vmem((2, per_row, LANES), F32),
        vmem((LINE, per_row, LANES), F32),
        vmem((8, LANES), F32),
        vmem((LINE, 8, LANES), F32),
        vmem((8, LANES), F32),
        vmem((YN, 8, LANES), F32),
        vmem((8, LANES), F32),
        vmem((zn, 8, LANES), F32),
        pltpu.SemaphoreType.DMA((states + 5,)),
        pltpu.SemaphoreType.DMA((n_sems,)),
        pltpu.SemaphoreType.DMA((n_sems,)),
    ]
    return pl.pallas_call(
        functools.partial(kernel, zn),
        out_shape=jax.ShapeDtypeStruct(control.shape, F32),
        in_specs=[pl.BlockSpec(memory_space=pltpu.SMEM)] + [any_] * 6,
        out_specs=pl.BlockSpec(memory_space=pltpu.VMEM),
        scratch_shapes=scratch,
        compiler_params=pltpu.CompilerParams(
            collective_id=0, has_side_effects=True, vmem_limit_bytes=60 * 1024 * 1024
        ),
    )(section_index, checkpoints, targets, sea_mask, basis_rows, basis_cols, control)


def solution(mesh):
    return jax.shard_map(
        on_device,
        mesh=mesh,
        in_specs=(
            P("ens", None, None, "space", None),
            P("ens"),
            P("ens", "space", None),
            P("space", None),
            P("space", None),
            P(),
            P("space", None),
        ),
        out_specs=P("space", None),
        check_vma=False,
    )
```

```python
import functools

import jax
import jax.numpy as jnp
from jax import lax
from jax.experimental import pallas as pl
from jax.experimental.pallas import tpu as pltpu
from jax.sharding import PartitionSpec as P

MESH = pl.DeviceIdType.MESH
F32 = jnp.float32
BF16 = jnp.bfloat16
EPSILON = 1e-06
LANES = 128
LINE = 8
ENS = 4
YN = 4
EARLY = 2
FOLD = 4


def kernel(
    zn,
    si_ref, ck_hbm, tg_hbm, mask_hbm, br_hbm, bc_hbm, ct_hbm, out_ref,
    ck, tg, mk_in, br, bc, ct, bcp, xin,
    ctl_s, ctl_g, ext, bhal, hs, hr, mk, tmp,
    hm_s, fx_s, fy_s, ab_s, cfs, cfg, pot, px, py, gx, gy,
    gs, gr, ps, pr, g_s, g_n, gfr, gyr, gy_s, gzr, fs, fr, sls, slr, sys_, syr, szs, szr,
    load_sem, send_sem, recv_sem,
):
    states, rows, cols = ck.shape[0], ck.shape[3], ck.shape[4]
    ring = rows + 8
    nk = cols // LANES
    basis = br.shape[1]
    piece = cols // ENS
    e = lax.axis_index("ens")
    t = lax.axis_index("space")
    x = t // (zn * YN)
    z = (t // YN) % zn
    y = t % YN
    j = x * ENS + e
    count = 2 * zn * YN

    def dev(e2, x2, z2, y2):
        return (e2, (x2 * zn + z2) * YN + y2)

    line = []
    for d in range(1, LINE):
        j2 = (j + d) % LINE
        line.append((j2, dev(j2 % ENS, j2 // ENS, z, y)))
    ys = []
    for d in range(1, YN):
        y2 = (y + d) % YN
        ys.append((y2, dev(e, x, z, y2)))
    zs = []
    for d in range(1, zn):
        z2 = (z + d) % zn
        zs.append((z2, dev(e, x, z2, y)))
    xzs = []
    for d in range(1, 2 * zn):
        q2 = (x * zn + z + d) % (2 * zn)
        xzs.append((q2, dev(e, q2 // zn, q2 % zn, y)))
    es = []
    for d in range(1, ENS):
        e2 = (e + d) % ENS
        es.append((e2, (e2, t)))
    partner = dev(e, 1 - x, z, y)
    after = (e, (t + 1) % count)
    before = (e, (t + count - 1) % count)

    base = [0]

    def sems(n):
        at = base[0]
        base[0] += n
        return at

    moves = [(ct_hbm, ct), (br_hbm, br)]
    moves += [(ck_hbm.at[i], ck.at[i]) for i in range(states)]
    moves += [(tg_hbm, tg), (mask_hbm, mk_in), (bc_hbm, bc)]
    loads = [pltpu.make_async_copy(src, dst, load_sem.at[i]) for i, (src, dst) in enumerate(moves)]
    for load in loads:
        load.start()
    n_ck = 2

    barrier = pltpu.get_barrier_semaphore()
    greet = [d for _, d in xzs + line + ys] + [after, before]
    for d in greet:
        pl.semaphore_signal(barrier, inc=1, device_id=d, device_id_type=MESH)

    def copy(src, dst, at_send, at_recv, device):
        return pltpu.make_async_remote_copy(
            src_ref=src,
            dst_ref=dst,
            send_sem=send_sem.at[at_send],
            recv_sem=recv_sem.at[at_recv],
            device_id=device,
            device_id_type=MESH,
        )

    sent = []

    def exchange(peers, me, n, src_of, dst_of):
        at = sems(n)
        for i, (p, device) in enumerate(peers):
            c = copy(src_of(p), dst_of(me), at + i, at + me, device)
            c.start()
            sent.append(c)

        def wait():
            for p, device in peers:
                copy(src_of(p), dst_of(p), at, at + p, device).wait_recv()

        return wait

    def single(src, dst, device):
        at = sems(1)
        c = copy(src, dst, at, at, device)
        c.start()
        sent.append(c)
        return c.wait_recv

    loads[0].wait()
    for b in range(LINE):
        ctl_s[b] = ct[:, b * LANES : (b + 1) * LANES].astype(BF16)
    ctl_g[x, z, y] = ctl_s[j]

    pl.semaphore_wait(barrier, len(greet))
    axz = exchange(
        xzs, x * zn + z, 2 * zn,
        lambda p: ctl_s.at[(p // zn) * ENS + e],
        lambda p: ctl_g.at[p // zn, p % zn, y],
    )
    loads[1].wait()
    top_rows = single(br.at[0:16], bhal.at[0], before)
    end_rows = single(br.at[rows - 16 : rows], bhal.at[1], after)

    sub = lax.broadcasted_iota(jnp.int32, (8, cols), 0)

    def tiles(s, field, first):
        at_rows = slice(first, first + 16)
        block = jnp.where(
            si_ref[s] == 0, ck[s, 0, field, at_rows, :].astype(F32), ck[s, 1, field, at_rows, :].astype(F32)
        )
        return block[0:8] if first == 0 else block[8:16]

    last = rows - 16
    edges = []
    for half in range(states // 2):
        if half == EARLY:
            axz()
            ay = exchange(ys, y, YN, lambda p: ctl_g.at[:, :, y], lambda p: ctl_g.at[:, :, p])
        up, down = [], []
        for s in (2 * half, 2 * half + 1):
            loads[n_ck + s].wait()
            h, u, v = (tiles(s, f, 0) for f in range(3))
            up.append(jnp.where(sub < 3, h, jnp.where(sub < 6, pltpu.roll(v, 3, 0), pltpu.roll(u, 6, 0))))
            h, u, v = (tiles(s, f, last) for f in range(3))
            down.append(jnp.where(sub >= 5, h, jnp.where(sub >= 2, pltpu.roll(v, 5, 0), pltpu.roll(u, 2, 0))))
        hs[0, half] = jnp.concatenate(up, axis=0).astype(BF16)
        hs[1, half] = jnp.concatenate(down, axis=0).astype(BF16)
        edges.append(single(hs.at[0, half], hr.at[0, half], before))
        edges.append(single(hs.at[1, half], hr.at[1, half], after))
    loads[n_ck + states].wait()
    loads[n_ck + states + 1].wait()
    up = jnp.zeros((8, cols), F32)
    down = jnp.zeros((8, cols), F32)
    for s in range(states):
        first = tg[s, 0:16, :].astype(F32)[0:8]
        up = jnp.where(sub == s, first if s == 0 else pltpu.roll(first, s, 0), up)
        final = tg[s, last : last + 16, :].astype(F32)[8:16]
        down = jnp.where(sub == s, final if s == 7 else pltpu.roll(final, s + 1, 0), down)
    half = states // 2
    hs[0, half] = jnp.concatenate([up, mk_in[0:8, :].astype(F32)], axis=0).astype(BF16)
    hs[1, half] = jnp.concatenate([down, mk_in[rows - 8 : rows, :].astype(F32)], axis=0).astype(BF16)
    edges.append(single(hs.at[0, half], hr.at[0, half], before))
    edges.append(single(hs.at[1, half], hr.at[1, half], after))

    wide = FOLD * LANES
    groups = cols // wide
    source = lax.broadcasted_iota(jnp.int32, (wide, wide), 0)
    place = lax.broadcasted_iota(jnp.int32, (wide, wide), 1)
    fold = (source == FOLD * (place % LANES) + place // LANES).astype(F32).astype(BF16)

    def folded(blocks):
        lhs = jnp.concatenate([b[:, g * wide : (g + 1) * wide] for g in range(groups) for b in blocks], axis=0)
        res = jnp.dot(lhs, fold, preferred_element_type=F32)
        high = blocks[0].shape[0]
        n = len(blocks)
        return [
            [res[(g * n + i) * high : (g * n + i + 1) * high] for g in range(groups)] for i in range(n)
        ]

    low_end = jnp.where(t < count - 1, 4, 0)
    high_start = jnp.where(t > 0, 4, 8)

    top_rows()
    end_rows()
    subb = lax.broadcasted_iota(jnp.int32, (8, basis), 0)
    edge = jnp.where(
        subb < low_end,
        bhal[0].astype(F32)[0:8],
        jnp.where(subb >= high_start, bhal[1].astype(F32)[8:16], 0.0),
    )
    ext[x, 0:rows] = br[...]
    ext[x, rows : rows + 16] = jnp.concatenate([edge, jnp.zeros_like(edge)], axis=0).astype(BF16)
    other_ext = single(ext.at[x], ext.at[x], partner)

    def own_rows(s, carry):
        slot = si_ref[s]
        parts = folded([ck[s, slot, 0], ck[s, slot, 1], ck[s, slot, 2], tg[s]])
        for i in range(4):
            for g in range(groups):
                xin[s, i, 0:rows, g * wide : (g + 1) * wide] = parts[i][g]
        return carry

    lax.fori_loop(0, states, own_rows, 0)
    (parts,) = folded([mk_in[...].astype(F32).astype(BF16)])
    for g in range(groups):
        mk[0:rows, g * wide : (g + 1) * wide] = parts[g]

    loads[n_ck + states + 2].wait()
    fold_t = (place == FOLD * (source % LANES) + source // LANES).astype(F32).astype(BF16)

    def basis_group(g, carry):
        at_g = pl.ds(pl.multiple_of(g * wide, wide), wide)
        bcp[at_g, :] = jnp.dot(fold_t, bc[at_g, :], preferred_element_type=F32).astype(BF16)
        return carry

    lax.fori_loop(0, groups, basis_group, 0)

    other_ext()
    ay()
    control_all = ctl_g[...].reshape(basis, LANES)
    lhs = ext[...].reshape(2 * (rows + 16), basis)
    cf = jnp.dot(lhs, control_all, preferred_element_type=F32).astype(BF16)
    cfs[...] = cf.reshape(2, rows + 16, LANES)
    cfg[j] = cfs[x]
    wait_cf = exchange(line, j, LINE, lambda p: cfs.at[p // ENS], lambda p: cfg.at[p])

    for wait_edge in edges:
        wait_edge()
    subw = lax.broadcasted_iota(jnp.int32, (8, wide), 0)

    def joined(low, high):
        return jnp.where(subw < low_end, low, jnp.where(subw >= high_start, high, 0.0))

    for half in range(states // 2 + 1):
        low4, high4 = folded([hr[0, half], hr[1, half]])
        for g in range(groups):
            at_g = slice(g * wide, (g + 1) * wide)
            low2, high2 = low4[g], high4[g]
            if half < states // 2:
                for i in range(2):
                    s = 2 * half + i
                    low, high = low2[8 * i : 8 * i + 8], high2[8 * i : 8 * i + 8]
                    xin[s, 0, rows:ring, at_g] = joined(low, high)
                    xin[s, 1, rows:ring, at_g] = joined(pltpu.roll(low, 2, 0), pltpu.roll(high, 6, 0))
                    xin[s, 2, rows:ring, at_g] = joined(pltpu.roll(low, 5, 0), pltpu.roll(high, 3, 0))
            else:
                for s in range(states):
                    low, high = low2[0:8], high2[0:8]
                    low = low if s == 0 else pltpu.roll(low, 8 - s, 0)
                    high = high if s == 7 else pltpu.roll(high, 7 - s, 0)
                    xin[s, 3, rows:ring, at_g] = joined(low, high)
                mk[rows:ring, at_g] = joined(low2[8:16], high2[8:16])

    lane = lax.broadcasted_iota(jnp.int32, (ring, LANES), 1)
    is_first = lane == 0
    is_last = lane == LANES - 1

    def row_diff(q):
        return pltpu.roll(q, ring - 1, 0) - pltpu.roll(q, 1, 0)

    def column_diff(get, k, turned):
        g, p = divmod(k, FOLD)

        def left(c):
            if c not in turned:
                turned[c] = pltpu.roll(get(c), LANES - 1, 1)
            return turned[c]

        def right(c):
            if c not in turned:
                turned[c] = pltpu.roll(get(c), 1, 1)
            return turned[c]

        if p < FOLD - 1:
            plus = get(k + 1)
        else:
            plus = jnp.where(is_last, left(k + 1) if g < groups - 1 else 0.0, left(k - p))
        if p > 0:
            minus = get(k - 1)
        else:
            minus = jnp.where(is_first, right(k - 1) if g > 0 else 0.0, right(k + FOLD - 1))
        return plus - minus

    def at(k):
        return slice(k * LANES, (k + 1) * LANES)

    def chunks(g):
        return range(g * FOLD, (g + 1) * FOLD)

    def before_stress(s, carry):
        fxt, ht = {}, {}
        for step in range(groups + 1):
            if step < groups:
                for k in chunks(step):
                    tmp[0, :, at(k)] = (1.0 + xin[s, 0, :, at(k)]) * xin[s, 1, :, at(k)]
            if step >= 1:
                for k in chunks(step - 1):
                    h, u, v, seen = (xin[s, f, :, at(k)] for f in range(4))
                    g = 1.0 + h
                    w = 0.15 * (column_diff(lambda c: tmp[0, :, at(c)], k, fxt) + row_diff(g * v))
                    hm = mk[:, at(k)] * (g - w)
                    dxh = column_diff(lambda c: xin[s, 0, :, at(c)], k, ht)
                    hm_s[s, :, at(k)] = hm
                    fx_s[s, :, at(k)] = hm * (0.97 * u + 0.15 * (v - dxh))
                    fy_s[s, :, at(k)] = hm * (0.97 * v - 0.15 * (u + row_diff(h)))
                    ab_s[s, :, at(k)] = 2.0 * (h - seen) - w
        return carry

    lax.fori_loop(0, states, before_stress, 0)

    wait_cf()
    coeffs = jnp.concatenate([cfg[b] for b in range(LINE)], axis=1)
    pot[...] = lax.dot_general(
        coeffs, bcp[...], (((1,), (1,)), ((), ())), preferred_element_type=F32
    )
    turns = {}
    for k in range(nk):
        px[:, at(k)] = -0.15 * row_diff(pot[0:ring, at(k)])
        py[:, at(k)] = 0.15 * column_diff(lambda c: pot[0:ring, at(c)], k, turns)
    gx[...] = jnp.zeros_like(gx)
    gy[...] = jnp.zeros_like(gy)

    def with_stress(s, carry):
        ft, at_ = {}, {}
        for step in range(groups + 2):
            if step < groups:
                for k in chunks(step):
                    tmp[0, :, at(k)] = fx_s[s, :, at(k)] + hm_s[s, :, at(k)] * px[:, at(k)]
            if 1 <= step <= groups:
                for k in chunks(step - 1):
                    dyf = row_diff(fy_s[s, :, at(k)] + hm_s[s, :, at(k)] * py[:, at(k)])
                    dxf = column_diff(lambda c: tmp[0, :, at(c)], k, ft)
                    tmp[1, :, at(k)] = mk[:, at(k)] * (ab_s[s, :, at(k)] - 0.15 * (dxf + dyf))
            if step >= 2:
                for k in chunks(step - 2):
                    hm = hm_s[s, :, at(k)]
                    gx[:, at(k)] += hm * column_diff(lambda c: tmp[1, :, at(c)], k, at_)
                    gy[:, at(k)] += hm * row_diff(tmp[1, :, at(k)])
        return carry

    lax.fori_loop(0, states, with_stress, 0)

    turns = {}
    per = piece // LANES
    at_e = sems(ENS)

    def to_ens(p, device):
        return copy(gs.at[p], gr.at[e], at_e + p, at_e + e, device)

    def quarter(p):
        @pl.when(e != p)
        def _():
            to_ens(p, (p, t)).start()

    for k in range(nk):
        dyg = column_diff(lambda c: gy[:, at(c)], k, turns)
        value = 0.005625 * (row_diff(gx[:, at(k)]) - dyg)
        gs[k // per, :, at(k % per)] = value[0:rows]
        if k % per == per - 1:
            quarter(k // per)

    gr[e] = gs[e]
    for p, device in es:
        copy(gs.at[p], gr.at[p], at_e, at_e + p, device).wait_recv()
        sent.append(to_ens(p, device))
    summed = ((gr[0] + gr[1]) + (gr[2] + gr[3])).astype(BF16)
    part = jnp.dot(summed, bcp[pl.ds(pl.multiple_of(e * piece, piece), piece), :], preferred_element_type=F32)
    for b in range(LINE):
        ps[b] = part[:, b * LANES : (b + 1) * LANES]
    pr[j] = ps[j]
    exchange(line, j, LINE, lambda p: ps.at[p], lambda p: pr.at[p])()
    projected = jnp.concatenate(
        [((pr[0] + pr[1]) + (pr[2] + pr[3])), ((pr[4] + pr[5]) + (pr[6] + pr[7]))], axis=0
    ).astype(BF16)

    rows2 = ext[:, 0:rows, :].reshape(2 * rows, basis)
    g_s[...] = lax.dot_general(
        rows2, projected, (((0,), (0,)), ((), ())), preferred_element_type=F32
    ).reshape(g_s.shape)
    g_n[...] = g_s[:, :, ys[1][0]].astype(BF16)
    order = [zn // 2]
    for d in range(zn // 2 - 1, 0, -1):
        order += [zn // 2 - (zn // 2 - d), zn - d]
    order.append(0)
    arrivals = {}
    for off in order:
        z2 = (z + off) % zn
        far = single(g_n.at[:, z2], gfr.at[off], ys[1][1])
        near = exchange(
            (ys[0], ys[2]), y, YN,
            lambda p, z2=z2: g_s.at[:, z2, p],
            lambda p, off=off: gyr.at[off, p],
        )
        arrivals[off] = (far, near)
    at_z = sems(zn)
    for i, off in enumerate(order):
        z2 = (z + off) % zn
        for wait in arrivals[off]:
            wait()
        total = (gyr[off, ys[0][0]] + gyr[off, ys[2][0]]) + (g_s[:, z2, y] + gfr[off].astype(F32))
        if off:
            gy_s[off] = total
            c = copy(gy_s.at[off], gzr.at[z], at_z + i, at_z + z, dev(e, x, z2, y))
            c.start()
            sent.append(c)
        else:
            gzr[z] = total
    for p, device in zs:
        copy(gy_s.at[0], gzr.at[p], at_z, at_z + p, device).wait_recv()
    total = gzr[0]
    for p in range(1, zn):
        total = total + gzr[p]

    per_row = total.shape[1]
    squares = total * total
    flat = squares.reshape(2 * per_row // 8, 8, LANES)
    square = flat[0]
    for i in range(1, 2 * per_row // 8):
        square = square + flat[i]
    sls[...] = square
    slr[j] = square
    line_squares = exchange(line, j, LINE, lambda p: sls, lambda p: slr.at[p])
    fs[...] = total
    fr[j] = fs[x]
    line_rows = exchange(line, j, LINE, lambda p: fs.at[p // ENS], lambda p: fr.at[p])
    line_squares()
    square = slr[0]
    for b in range(1, LINE):
        square = square + slr[b]
    sys_[...] = square
    syr[y] = square
    exchange(ys, y, YN, lambda p: sys_, lambda p: syr.at[p])()
    square = (syr[0] + syr[1]) + (syr[2] + syr[3])
    szs[...] = square
    szr[z] = square
    early = list(sent)
    wait_squares = exchange(zs, z, zn, lambda p: szs, lambda p: szr.at[p])
    line_rows()
    gradient = jnp.concatenate([fr[b] for b in range(LINE)], axis=1)
    for c in early:
        c.wait_send()
    wait_squares()
    square = szr[0]
    for b in range(1, zn):
        square = square + szr[b]
    mean = jnp.sum(square, keepdims=True) / (basis * basis)
    root = jnp.sqrt(mean + EPSILON)
    out_ref[...] = ct[...] - gradient / root

    for c in sent[len(early) :]:
        c.wait_send()


def on_device(checkpoints, section_index, targets, sea_mask, basis_rows, basis_cols, control):
    states, slots, fields, rows, cols = checkpoints.shape
    basis = basis_cols.shape[1]
    per_row = control.shape[0]
    count = lax.axis_size("space")
    zn = count // (2 * YN)
    ring = rows + 8
    n_sems = 2 * zn + 2 + 2 * (states // 2 + 1) + 1 + YN + LINE + ENS + LINE + zn * (YN + 1) + zn + 2 * LINE + YN + zn
    any_ = pl.BlockSpec(memory_space=pl.ANY)
    vmem = pltpu.VMEM
    scratch = [
        vmem((states, slots, fields, rows, cols), BF16),
        vmem((states, rows, cols), BF16),
        vmem((rows, cols), jnp.int32),
        vmem((rows, basis), BF16),
        vmem((cols, basis), BF16),
        vmem((per_row, basis), F32),
        vmem((cols, basis), BF16),
        vmem((states, 4, ring, cols), F32),
        vmem((LINE, per_row, LANES), BF16),
        vmem((2, zn, YN, per_row, LANES), BF16),
        vmem((2, rows + 16, basis), BF16),
        vmem((2, 16, basis), BF16),
        vmem((2, states // 2 + 1, 16, cols), BF16),
        vmem((2, states // 2 + 1, 16, cols), BF16),
        vmem((ring, cols), F32),
        vmem((2, ring, cols), F32),
        vmem((states, ring, cols), F32),
        vmem((states, ring, cols), F32),
        vmem((states, ring, cols), F32),
        vmem((states, ring, cols), F32),
        vmem((2, rows + 16, LANES), BF16),
        vmem((LINE, rows + 16, LANES), BF16),
        vmem((rows + 16, cols), F32),
        vmem((ring, cols), F32),
        vmem((ring, cols), F32),
        vmem((ring, cols), F32),
        vmem((ring, cols), F32),
        vmem((ENS, rows, cols // ENS), F32),
        vmem((ENS, rows, cols // ENS), F32),
        vmem((LINE, rows, LANES), F32),
        vmem((LINE, rows, LANES), F32),
        vmem((2, zn, YN, per_row, LANES), F32),
        vmem((2, zn, per_row, LANES), BF16),
        vmem((zn, 2, per_row, LANES), BF16),
        vmem((zn, YN, 2, per_row, LANES), F32),
        vmem((zn, 2, per_row, LANES), F32),
        vmem((zn, 2, per_row, LANES), F32),
        vmem((2, per_row, LANES), F32),
        vmem((LINE, per_row, LANES), F32),
        vmem((8, LANES), F32),
        vmem((LINE, 8, LANES), F32),
        vmem((8, LANES), F32),
        vmem((YN, 8, LANES), F32),
        vmem((8, LANES), F32),
        vmem((zn, 8, LANES), F32),
        pltpu.SemaphoreType.DMA((states + 5,)),
        pltpu.SemaphoreType.DMA((n_sems,)),
        pltpu.SemaphoreType.DMA((n_sems,)),
    ]
    return pl.pallas_call(
        functools.partial(kernel, zn),
        out_shape=jax.ShapeDtypeStruct(control.shape, F32),
        in_specs=[pl.BlockSpec(memory_space=pltpu.SMEM)] + [any_] * 6,
        out_specs=pl.BlockSpec(memory_space=pltpu.VMEM),
        scratch_shapes=scratch,
        compiler_params=pltpu.CompilerParams(
            collective_id=0, has_side_effects=True, vmem_limit_bytes=60 * 1024 * 1024
        ),
    )(section_index, checkpoints, targets, sea_mask, basis_rows, basis_cols, control)


def solution(mesh):
    return jax.shard_map(
        on_device,
        mesh=mesh,
        in_specs=(
            P("ens", None, None, "space", None),
            P("ens"),
            P("ens", "space", None),
            P("space", None),
            P("space", None),
            P(),
            P("space", None),
        ),
        out_specs=P("space", None),
        check_vma=False,
    )
```
